32 devices in a mesh: tier: 4 (over x, core), tile: 8 (over z, y).
Axes of the slice: x: 2, y: 2, z: 4, core: 2. Of those that a mesh axis runs over, the one named last changes fastest.
Arguments:
- starting_warmth_rise: float32 [32, 96, 1024], P('tile', 'tier'), may hold values from -3 to 8
- substance_per_cell: int32 [32, 96, 1024], P('tile', 'tier'), may hold values from 0 to 7
- material_transport_rates: float32 [2, 8], replicated, may hold values from 0.2 to 2
- patch_region_label: int32 [8, 8], P('tile'), may hold values from 0 to 15, as said below
- static_power_per_area: float32 [4, 16], replicated, may hold values from 0.5 to 4
- warming_power_factor: float32 [4, 16], replicated, may hold values from 0.2 to 0.8
- stacking_solve_operator: float32 [96, 96], replicated, may hold values from 0 to 1
Outputs:
- final_temperature: float32 [32, 96, 1024], P('tile', 'tier')
- block_power: float32 [4, 16], P('tier')
The draws below stay inside these ranges and needn't reach their ends.
Inputs may be any that keep to these rules, and one draw needn't show every extreme that they name: `patch_region_label`: every block number names at least one tile.
All inputs are finite; a program needn't handle non-finite values.
Results may differ from the reference program's by a relative error of at most 0.0001.
Values sent between devices are 32-bit elements; how exact they have to be, the bound alone decides.
A program may use at most 64 MiB of HBM per device.

```python
import math
import jax
import jax.numpy as jnp
from jax import lax

ROWS = 4
NY = 1024
LEVELS = 96
TILE_COLS = 128
NMAT = 8
STEPS = 2
TIERS = 4
LEV = 24
NX = 32
NBLK = 16


def draw_starting_warmth_rise(key, part):
    key_one, key_two = jax.random.split(jax.random.fold_in(key, 11))
    ramp_up = (1.0 + 2.0 * jnp.arange(NX, dtype=jnp.float32) / (NX - 1))[:, None, None]
    rough_part = jax.random.uniform(key_one, (NX, LEVELS, NY), jnp.float32, 0.5, 1.5)
    noise_part = 0.3 * jnp.clip(jax.random.normal(key_two, (NX, LEVELS, NY), jnp.float32), -6.0, 6.0)
    return ramp_up * rough_part + noise_part


def draw_patch_region_label(key, part):
    key_one, key_two = jax.random.split(jax.random.fold_in(key, 23))
    tile_total = NX // ROWS * (NY // TILE_COLS)
    positions = jnp.arange(tile_total, dtype=jnp.int32)
    extra_ids = jax.random.randint(key_one, (tile_total,), 0, NBLK, dtype=jnp.int32)
    tile_ids = jnp.where(positions < NBLK, positions, extra_ids)
    shuffle = jax.random.permutation(key_two, tile_total)
    return tile_ids[shuffle].reshape(NX // ROWS, NY // TILE_COLS)


def draw_stacking_solve_operator(key, part):
    levels_pos = jnp.arange(LEVELS, dtype=jnp.float32)
    distance = jnp.abs(levels_pos[:, None] - levels_pos[None, :])
    kernel = jnp.exp(-distance / (2.0 * LEV))
    rough_part = jax.random.uniform(jax.random.fold_in(key, 37), (LEVELS, LEVELS), jnp.float32, 0.5, 1.5)
    scale_off = 0.45 / (1.5 * (1.0 + 4.0 * LEV))
    return scale_off * kernel * rough_part + 0.5 * jnp.eye(LEVELS, dtype=jnp.float32)


def touch_ends(values, key, smallest, high):
    longest = values.shape.index(max(values.shape))
    spots = []
    for shift in (0, 1):
        where = [jax.random.randint(jax.random.fold_in(key, axis), (), 0, length) for axis, length in enumerate(values.shape)]
        where[longest] = (where[longest] + shift) % values.shape[longest]
        spots.append(tuple(where))
    return values.at[spots[0]].set(smallest).at[spots[1]].set(high)


def setup_inputs(seed: int = 0) -> dict:
    key_list = jax.random.split(jax.random.key(seed), 8)
    starting_warmth_rise = draw_starting_warmth_rise(jax.random.fold_in(key_list[7], 71), 0)
    substance_per_cell = touch_ends(jax.random.randint(key_list[1], (NX, LEVELS, NY), 0, NMAT), jax.random.fold_in(key_list[1], 1), 0, NMAT - 1).astype(jnp.int32)
    material_transport_rates = jnp.clip(jnp.exp(jax.random.uniform(key_list[2], (2, NMAT), jnp.float32, math.log(0.2), math.log(2.0))), 0.2, 2.0)
    patch_region_label = draw_patch_region_label(jax.random.fold_in(key_list[7], 71), 0)
    static_power_per_area = jnp.clip(jnp.exp(jax.random.uniform(key_list[4], (TIERS, NBLK), jnp.float32, math.log(0.5), math.log(4.0))), 0.5, 4.0)
    warming_power_factor = jnp.clip(jax.random.uniform(key_list[5], (TIERS, NBLK), jnp.float32, 0.2, 0.8), 0.2, 0.8)
    stacking_solve_operator = draw_stacking_solve_operator(jax.random.fold_in(key_list[7], 71), 0)
    return dict(starting_warmth_rise=starting_warmth_rise, substance_per_cell=substance_per_cell, material_transport_rates=material_transport_rates, patch_region_label=patch_region_label, static_power_per_area=static_power_per_area, warming_power_factor=warming_power_factor, stacking_solve_operator=stacking_solve_operator)


LATERAL_RATE = 0.12
SOURCE_GAIN = 0.02


def pair_mean(cond_a, cond_b):
    return 2.0 * cond_a * cond_b / (cond_a + cond_b)


def lateral(padded, conduct):
    centre = padded[1:-1, :, 1:-1]
    sideways_coupling_rate = conduct[0, 1:-1, :, 1:-1]
    stacking_coupling_rate = conduct[1, 1:-1, :, 1:-1]
    flow_sum = pair_mean(sideways_coupling_rate, conduct[0, 2:, :, 1:-1]) * (padded[2:, :, 1:-1] - centre)
    flow_sum = flow_sum + pair_mean(sideways_coupling_rate, conduct[0, :-2, :, 1:-1]) * (padded[:-2, :, 1:-1] - centre)
    flow_sum = flow_sum + pair_mean(stacking_coupling_rate, conduct[1, 1:-1, :, 2:]) * (padded[1:-1, :, 2:] - centre)
    flow_sum = flow_sum + pair_mean(stacking_coupling_rate, conduct[1, 1:-1, :, :-2]) * (padded[1:-1, :, :-2] - centre)
    return centre + LATERAL_RATE * flow_sum


def reference(starting_warmth_rise, substance_per_cell, material_transport_rates, patch_region_label, static_power_per_area, warming_power_factor, stacking_solve_operator):
    sideways_coupling_rate = jnp.zeros(starting_warmth_rise.shape, jnp.float32)
    stacking_coupling_rate = jnp.zeros(starting_warmth_rise.shape, jnp.float32)
    for material in range(NMAT):
        is_material = substance_per_cell == material
        sideways_coupling_rate = jnp.where(is_material, material_transport_rates[0, material], sideways_coupling_rate)
        stacking_coupling_rate = jnp.where(is_material, material_transport_rates[1, material], stacking_coupling_rate)
    cond_pad = jnp.pad(jnp.stack([sideways_coupling_rate, stacking_coupling_rate]), ((0, 0), (1, 1), (0, 0), (1, 1)))
    tile_ids = patch_region_label.reshape(-1).astype(jnp.int32)
    tile_rows = NX // ROWS
    tile_cols = NY // TILE_COLS
    counts = jax.ops.segment_sum(jnp.ones(tile_ids.shape, jnp.float32), tile_ids, num_segments=NBLK) * float(ROWS * TILE_COLS)
    present_warming_state = starting_warmth_rise
    block_power = jnp.zeros((TIERS, NBLK), jnp.float32)
    for step_index in range(STEPS):
        active = present_warming_state[:, ::LEV, :]
        tile_sums = active.reshape(tile_rows, ROWS, TIERS, tile_cols, TILE_COLS).sum(axis=(1, 4))
        per_tile = jnp.transpose(tile_sums, (1, 0, 2)).reshape(TIERS, -1)
        block_sum = jax.vmap(lambda values: jax.ops.segment_sum(values, tile_ids, num_segments=NBLK))(per_tile)
        block_power = static_power_per_area * jnp.exp(warming_power_factor * block_sum / counts)
        tile_power = block_power[:, tile_ids].reshape(TIERS, tile_rows, tile_cols)
        cell_power = jnp.repeat(jnp.repeat(tile_power, ROWS, axis=1), TILE_COLS, axis=2)
        moved_field = lateral(jnp.pad(present_warming_state, ((1, 1), (0, 0), (1, 1))), cond_pad)
        moved_field = moved_field.at[:, ::LEV, :].add(SOURCE_GAIN * jnp.transpose(cell_power, (1, 0, 2)))
        present_warming_state = jnp.einsum("lm,xmy->xly", stacking_solve_operator, moved_field, precision=lax.Precision.HIGHEST)
    return present_warming_state, block_power
```

```python
import functools

import jax
import jax.numpy as jnp
from jax import lax
from jax.experimental import pallas as pl
from jax.experimental.pallas import tpu as pltpu
from jax.sharding import PartitionSpec as P

C = 128
RATE = 0.12
SOURCE_GAIN = 0.02
MESH = pl.DeviceIdType.MESH


def solve(op, x):
    return jnp.dot(op, x, precision=lax.Precision.HIGHEST, preferred_element_type=jnp.float32)


def roll(x, shift):
    return pltpu.roll(x, shift % C, x.ndim - 1) if shift % C else x


def kernel(
    ntier, ntile, nblk, group,
    t_hbm, m_hbm, rates_hbm, labels_hbm, stat_hbm, fac_hbm, a_hbm,
    out, pw_out,
    t_in, m_in, rates, labels, stat, fac, a_in, s_in,
    col_t, col_m, halo_t, halo_m, halo_1,
    pk_out, pk, halo_p,
    cx, cy, ce, mv, t1, t1c, res,
    p1g, p1z, p2g, p2z,
    s_t, s_m, s_pk, s_o,
    r_et, r_em, r_rt, r_rm, r_pk, r_o,
    s_h, r_h,
    s_p1g, r_p1g, s_p1z, r_p1z, s_p2g, r_p2g, s_p2z, r_p2z,
):
    tier = lax.axis_index("tier")
    tile = lax.axis_index("tile")
    rows, lev, width = t_in.shape
    levels = lev * ntier
    nmat = rates.shape[1]
    ngrp = ntile // group
    grows = rows * group
    sub = lax.rem(tile, group)
    base = tile - sub
    place = tile // group
    own = tier * group + sub
    nwin = ntier * group
    active_rows = [t * lev for t in range(ntier)]

    loads = [
        pltpu.make_async_copy(src, dst, s_in.at[i])
        for i, (src, dst) in enumerate(
            ((t_hbm, t_in), (m_hbm, m_in), (labels_hbm, labels), (rates_hbm, rates),
             (stat_hbm, stat), (fac_hbm, fac), (a_hbm, a_in))
        )
    ]
    for load in loads:
        load.start()

    peers = []
    for a in range(ntier):
        for b in range(group):
            t2 = lax.rem(tier + a, ntier)
            s2 = lax.rem(sub + b, group)
            peers.append((a == 0 and b == 0, t2, s2))

    def there(t2, s2):
        return {"tier": t2, "tile": base + s2}

    barrier = pltpu.get_barrier_semaphore()
    for mine, t2, s2 in peers:
        if not mine:
            pl.semaphore_signal(barrier, inc=1, device_id=there(t2, s2), device_id_type=MESH)

    def across(k):
        return {"tile": lax.rem(tile + k * group, ntile)}

    def greet(k, carry):
        pl.semaphore_signal(barrier, inc=1, device_id=across(k), device_id_type=MESH)
        return carry

    lax.fori_loop(1, ngrp, greet, 0)

    def cols(w):
        return pl.ds(pl.multiple_of(w * C, C), C)

    def levs(t):
        return pl.ds(pl.multiple_of(t * lev, 8), lev)

    lane = lax.broadcasted_iota(jnp.int32, (1, C), 1)
    blk = lax.broadcasted_iota(jnp.int32, (1, nblk), 1)

    for load in loads:
        load.wait()

    sums = jnp.zeros((1, nblk), jnp.float32)
    areas = jnp.zeros((1, nblk), jnp.float32)
    names = jnp.zeros((1, C), jnp.float32)
    active = t_in[0, 0:1, :]
    for r in range(1, rows):
        active = active + t_in[r, 0:1, :]
    for j in range(width // C):
        part = jnp.sum(active[:, j * C : (j + 1) * C], axis=1, keepdims=True)
        hit = blk == labels[0, j]
        sums = sums + jnp.where(hit, part, 0.0)
        areas = areas + jnp.where(hit, float(rows * C), 0.0)
        names = jnp.where(lane == j, labels[0, j].astype(jnp.float32), names)
    p1g[own] = jnp.zeros(p1g.shape[1:], jnp.float32)
    p1g[own, 0:1, 0:nblk] = sums
    p1g[own, 1:2, 0:nblk] = areas
    p1g[own, 2:3, 0:C] = names

    pl.semaphore_wait(barrier, nwin - 1 + ngrp - 1)

    def group_send(buf, s_sem, r_sem):
        for mine, t2, s2 in peers:
            if not mine:
                pltpu.make_async_remote_copy(
                    src_ref=buf.at[own], dst_ref=buf.at[own], send_sem=s_sem, recv_sem=r_sem,
                    device_id=there(t2, s2), device_id_type=MESH,
                ).start()

    def across_send(buf, s_sem, r_sem):
        def send(k, carry):
            pltpu.make_async_remote_copy(
                src_ref=buf.at[0], dst_ref=buf.at[k], send_sem=s_sem, recv_sem=r_sem,
                device_id=across(k), device_id_type=MESH,
            ).start()
            return carry

        lax.fori_loop(1, ngrp, send, 0)

    def wait_for(ref, sem):
        pltpu.make_async_copy(ref, ref, sem).wait()

    def all_but_one(buf, sem):
        wait_for(buf.at[pl.ds(1, buf.shape[0] - 1)], sem)

    def total(buf):
        return lax.fori_loop(1, ngrp, lambda k, acc: acc + buf[k], buf[0])

    group_send(p1g, s_p1g, r_p1g)

    def spread(src, dst, row, to, count, s_sem, r_sem):
        for mine, t2, s2 in peers:
            src_ref = src.at[pl.ds(row, count), :, cols(t2 * group + s2)]
            dst_ref = dst.at[pl.ds(to, count), levs(tier), :]
            if mine:
                pltpu.make_async_copy(src_ref, dst_ref, r_sem).start()
            else:
                pltpu.make_async_remote_copy(
                    src_ref=src_ref, dst_ref=dst_ref, send_sem=s_sem, recv_sem=r_sem,
                    device_id=there(t2, s2), device_id_type=MESH,
                ).start()

    edge = lax.select(sub == 0, 0, rows - 1)
    rest = lax.select(sub == 0, 1, 0)
    spread(t_hbm, col_t, edge, sub * rows + edge, 1, s_t, r_et.at[sub])
    spread(m_hbm, col_m, edge, sub * rows + edge, 1, s_m, r_em.at[sub])

    quad = lane >> 2
    for w in range(nwin):
        low = max(w - 1, 0) * C
        high = min(w + 1, nwin - 1) * C
        for g in range(lev // 8):
            ls = slice(8 * g, 8 * g + 8)
            acc = None
            for q, src in ((0, t_in), (rows, m_in)):
                for r in range(rows):
                    both = jnp.where(
                        lane >= 64, src[r, ls, low : low + C], src[r, ls, high : high + C]
                    )
                    if q:
                        both = both.astype(jnp.float32)
                    put = roll(both, 32 * g + 4 * (q + r) + 2)
                    acc = put if acc is None else jnp.where(quad == 8 * g + q + r, put, acc)
            pk_out[w, g] = acc

    def fold(w):
        total_p = None
        for g in range(lev // 8):
            piece = pk_out[w, g]
            keep = (lane >= 32 * g) & (lane < 32 * g + 32)
            total_p = jnp.where(keep, piece, 0.0) if total_p is None else jnp.where(keep, piece, total_p)
        return total_p

    for w in range(nwin):
        pk_out[w, 0] = fold(w)

    for mine, t2, s2 in peers:
        src_ref, dst_ref = pk_out.at[t2 * group + s2, 0], pk.at[sub, tier]
        if mine:
            pltpu.make_async_copy(src_ref, dst_ref, r_pk).start()
        else:
            pltpu.make_async_remote_copy(
                src_ref=src_ref, dst_ref=dst_ref, send_sem=s_pk, recv_sem=r_pk,
                device_id=there(t2, s2), device_id_type=MESH,
            ).start()
    spread(m_hbm, col_m, rest, sub * rows + rest, rows - 1, s_m, r_rm)
    spread(t_hbm, col_t, rest, sub * rows + rest, rows - 1, s_t, r_rt)

    has_low = place > 0
    has_high = place < ngrp - 1

    @pl.when(jnp.logical_not(has_low))
    def _():
        for ref in (halo_t, halo_m, halo_p, halo_1):
            ref[0] = jnp.zeros(ref.shape[1:], ref.dtype)

    @pl.when(jnp.logical_not(has_high))
    def _():
        for ref in (halo_t, halo_m, halo_p, halo_1):
            ref[1] = jnp.zeros(ref.shape[1:], ref.dtype)

    def halo(low_src, high_src, dst, which):
        down = pltpu.make_async_remote_copy(
            src_ref=low_src, dst_ref=dst.at[1],
            send_sem=s_h.at[which, 0], recv_sem=r_h.at[which, 1],
            device_id={"tile": lax.max(tile - group, sub)}, device_id_type=MESH,
        )
        up = pltpu.make_async_remote_copy(
            src_ref=high_src, dst_ref=dst.at[0],
            send_sem=s_h.at[which, 1], recv_sem=r_h.at[which, 0],
            device_id={"tile": lax.min(tile + group, ntile - group + sub)}, device_id_type=MESH,
        )
        return down, up

    def halo_recv(copies):
        pl.when(has_low)(lambda: copies[1].wait_recv())
        pl.when(has_high)(lambda: copies[0].wait_recv())

    def halo_sent(copies):
        pl.when(has_low)(lambda: copies[0].wait_send())
        pl.when(has_high)(lambda: copies[1].wait_send())

    h_t = halo(col_t.at[0], col_t.at[grows - 1], halo_t, 0)
    h_m = halo(col_m.at[0], col_m.at[grows - 1], halo_m, 1)
    h_p = halo(pk.at[0], pk.at[group - 1], halo_p, 2)
    h_1 = halo(t1.at[0], t1.at[grows - 1], halo_1, 3)

    all_but_one(p1g, r_p1g)
    p1z[0] = jnp.zeros(p1z.shape[1:], jnp.float32)
    for t in range(ntier):
        acc = p1g[t * group, 0:1, :]
        for s in range(1, group):
            acc = acc + p1g[t * group + s, 0:1, :]
        p1z[0, t : t + 1, :] = acc
    acc = p1g[0, 1:2, :]
    for s in range(1, group):
        acc = acc + p1g[s, 1:2, :]
    p1z[0, ntier : ntier + 1, :] = acc
    across_send(p1z, s_p1z, r_p1z)

    for s, row in ((0, 0), (group - 1, grows - 1)):
        wait_for(col_t.at[row], r_et.at[s])
        wait_for(col_m.at[row], r_em.at[s])
    pl.when(has_low)(lambda: (h_m[0].start(), h_t[0].start()) and None)
    pl.when(has_high)(lambda: (h_m[1].start(), h_t[1].start()) and None)
    wait_for(pk, r_pk)
    pl.when(has_low)(lambda: h_p[0].start())
    pl.when(has_high)(lambda: h_p[1].start())

    inverse = 1.0 / ((2.0 * RATE) * rates[...])
    table = [
        [jnp.broadcast_to(inverse[a : a + 1, m : m + 1], (1, C)) for m in range(nmat)]
        for a in range(2)
    ]

    def lookup(codes, axes):
        outs = [jnp.broadcast_to(table[a][0], codes.shape) for a in axes]
        for m in range(1, nmat):
            hit = codes == m
            outs = [jnp.where(hit, table[a][m], o) for a, o in zip(axes, outs)]
        return outs

    def unpack(low, high, shift_low, shift_high, split):
        pieces = []
        for t in range(ntier):
            for g in range(lev // 8):
                a = roll(low(t), shift_low - 32 * g)
                if high is not None:
                    a = jnp.where(lane < split, a, roll(high(t), shift_high - 32 * g))
                pieces.append(a)
        return jnp.concatenate(pieces, axis=0)

    def swap(x):
        return jnp.where((lane & 3) == 1, roll(x, -1), roll(x, 1))

    half = 4 * rows
    out_t = unpack(lambda t: pk[0, t], lambda t: pk[1, t], 0, half, half)
    out_m = unpack(lambda t: pk[0, t], lambda t: pk[1, t], -half, 0, half)
    ixc, iyc = lookup(out_m, (0, 1))
    pos_low = (lane & 3) == 1

    wait_for(col_m.at[pl.ds(1, grows - 2)], r_rm)
    before = None
    inner = jnp.ones((levels, C), jnp.float32)
    for r in range(grows):
        ix, iy = lookup(col_m[r], (0, 1))
        cy[r] = 1.0 / (iy + roll(iy, -1))
        inner = jnp.where((lane >> 2) == r, roll(iy, 4 * r + 2), inner)
        if r == 0:
            first = ix
        else:
            cx[r] = 1.0 / (before + ix)
        before = ix
    last = before

    there_is = jnp.where(pos_low, jnp.where(own > 0, 1.0, 0.0), jnp.where(own < nwin - 1, 1.0, 0.0))
    c_in = there_is / (iyc + swap(inner))
    c_far = 1.0 / (iyc + jnp.where(pos_low, roll(iyc, 1), roll(iyc, -1)))
    spun = swap(c_in)
    for r in range(grows):
        ce[r] = roll(spun, -(4 * r + 2))
        cy[r] = jnp.where(lane == C - 1, ce[r], cy[r])

    halo_recv(h_m)
    halo_recv(h_p)
    (ix,) = lookup(halo_m[0], (0,))
    cx[0] = jnp.where(has_low, 1.0 / (ix + first), 0.0)
    (ix,) = lookup(halo_m[1], (0,))
    cx[grows] = jnp.where(has_high, 1.0 / (ix + last), 0.0)

    end = 4 * (rows - 1)
    up_t = unpack(lambda t: halo_p[0, t], None, -end, 0, 0)
    up_m = unpack(lambda t: halo_p[0, t], None, -end - half, 0, 0)
    dn_t = unpack(lambda t: halo_p[1, t], None, 4 * (grows - 1), 0, 0)
    dn_m = unpack(lambda t: halo_p[1, t], None, 4 * (grows - 1) - half, 0, 0)
    (up_ix,) = lookup(up_m, (0,))
    (dn_ix,) = lookup(dn_m, (0,))
    at_top = lane < 4
    at_bottom = lane >= 4 * (grows - 1)
    up_c = 1.0 / (ixc + jnp.where(at_top, up_ix, roll(ixc, 4)))
    up_c = jnp.where(jnp.logical_and(at_top, jnp.logical_not(has_low)), 0.0, up_c)
    dn_c = 1.0 / (ixc + jnp.where(at_bottom, dn_ix, roll(ixc, -4)))
    dn_c = jnp.where(jnp.logical_and(at_bottom, jnp.logical_not(has_high)), 0.0, dn_c)
    part = (
        out_t
        + up_c * (jnp.where(at_top, up_t, roll(out_t, 4)) - out_t)
        + dn_c * (jnp.where(at_bottom, dn_t, roll(out_t, -4)) - out_t)
        + c_far * (jnp.where(pos_low, roll(out_t, 1), roll(out_t, -1)) - out_t)
    )

    op = a_in[...]
    op_active = [op[:, a : a + 1] for a in active_rows]

    all_but_one(p1z, r_p1z)
    whole = total(p1z)
    count = whole[ntier : ntier + 1, 0:nblk]
    power = stat[...] * jnp.exp(fac[...] * whole[0:ntier, 0:nblk] / count)

    def label_of(s, w):
        return jnp.sum(jnp.where(lane == w, p1g[s, 2:3, 0:C], 0.0), axis=1, keepdims=True)

    blkf = blk.astype(jnp.float32)

    def gain_of(pw, label):
        return SOURCE_GAIN * jnp.sum(jnp.where(blkf == label, pw, 0.0), axis=1, keepdims=True)

    own_labels = [label_of(s, own) for s in range(group)]
    gains = [gain_of(power, label) for label in own_labels]
    lift = []
    for s in range(group):
        acc = op_active[0] * gains[s][0:1, :]
        for t in range(1, ntier):
            acc = acc + op_active[t] * gains[s][t : t + 1, :]
        lift.append(acc)
    side = jnp.zeros((ntier, C), jnp.float32)
    for s in range(group):
        gl = gain_of(power, label_of(s, own - 1))
        gr = gain_of(power, label_of(s, own + 1))
        side = jnp.where(lane // half == s, jnp.where(pos_low, gl, gr), side)
    lift_c = op_active[0] * side[0:1, :]
    for t in range(1, ntier):
        lift_c = lift_c + op_active[t] * side[t : t + 1, :]

    def lateral(field, outside, r, above, below):
        here = field[r]
        edge_in = roll(outside, -(4 * r + 2))
        beside = jnp.where(lane == C - 1, edge_in, roll(here, -1))
        flux = cy[r] * (beside - here)
        left = jnp.where(lane == 0, ce[r] * (here - edge_in), roll(flux, 1))
        moved = here + (flux - left)
        return moved + cx[r + 1] * (below - here) - cx[r] * (here - above)

    halo_recv(h_t)
    wait_for(col_t.at[pl.ds(1, grows - 2)], r_rt)
    spun = swap(out_t)
    inner = out_t
    for r in range(grows):
        above = halo_t[0] if r == 0 else col_t[r - 1]
        below = halo_t[1] if r == grows - 1 else col_t[r + 1]
        mv[:, r * C : (r + 1) * C] = lateral(col_t, spun, r, above, below)
        inner = jnp.where((lane >> 2) == r, roll(col_t[r], 4 * r + 2), inner)
    mv[:, grows * C : (grows + 1) * C] = part + c_in * (swap(inner) - out_t)

    order = [0, grows - 1] + list(range(1, grows - 1))
    for r in order:
        t1[r] = solve(op, mv[:, r * C : (r + 1) * C]) + lift[r // rows]
        if r == grows - 1:
            pl.when(has_low)(lambda: h_1[0].start())
            pl.when(has_high)(lambda: h_1[1].start())
    t1c = solve(op, mv[:, grows * C : (grows + 1) * C]) + lift_c

    p2g[own] = jnp.zeros(p2g.shape[1:], jnp.float32)
    sums = jnp.zeros((ntier, nblk), jnp.float32)
    for s in range(group):
        acc = []
        for a in active_rows:
            v = t1[s * rows, a : a + 1, :]
            for r in range(1, rows):
                v = v + t1[s * rows + r, a : a + 1, :]
            acc.append(v)
        acc = jnp.sum(jnp.concatenate(acc, axis=0), axis=1, keepdims=True)
        sums = sums + jnp.where(blkf == own_labels[s], acc, 0.0)
    p2g[own, 0:ntier, 0:nblk] = sums
    group_send(p2g, s_p2g, r_p2g)

    def send_rows(s, first_row, count):
        for t in range(ntier):
            for_me = jnp.logical_and(tier == t, sub == s)
            src_ref = res.at[pl.ds(s * rows + first_row, count), pl.ds(t * lev, lev), :]
            dst_ref = out.at[pl.ds(first_row, count), :, cols(own)]

            @pl.when(for_me)
            def _():
                pltpu.make_async_copy(src_ref, dst_ref, r_o).start()

            @pl.when(jnp.logical_not(for_me))
            def _():
                pltpu.make_async_remote_copy(
                    src_ref=src_ref, dst_ref=dst_ref, send_sem=s_o, recv_sem=r_o,
                    device_id=there(t, s), device_id_type=MESH,
                ).start()

    spun = swap(t1c)

    def finish(r):
        above = halo_1[0] if r == 0 else t1[r - 1]
        below = halo_1[1] if r == grows - 1 else t1[r + 1]
        mv[:, r * C : (r + 1) * C] = lateral(t1, spun, r, above, below)
        res[r] = solve(op, mv[:, r * C : (r + 1) * C])

    for s in range(group):
        for r in range(s * rows + (s == 0), (s + 1) * rows - (s == group - 1)):
            finish(r)
        send_rows(s, int(s == 0), rows - 1)

    all_but_one(p2g, r_p2g)
    acc = p2g[0]
    for k in range(1, nwin):
        acc = acc + p2g[k]
    p2z[0] = acc
    across_send(p2z, s_p2z, r_p2z)

    halo_recv(h_1)
    for s, r in ((0, 0), (group - 1, grows - 1)):
        finish(r)
        send_rows(s, r - s * rows, 1)

    all_but_one(p2z, r_p2z)
    whole = total(p2z)
    power = stat[...] * jnp.exp(fac[...] * whole[0:ntier, 0:nblk] / count)
    mine = lax.broadcasted_iota(jnp.int32, (ntier, nblk), 0) == tier
    pw_out[...] = jnp.sum(jnp.where(mine, power, 0.0), axis=0, keepdims=True)
    own_op = a_in[levs(tier), :]
    lifts = []
    for j in range(width // C):
        g = SOURCE_GAIN * jnp.sum(jnp.where(blk == labels[0, j], power, 0.0), axis=1, keepdims=True)
        acc = own_op[:, active_rows[0] : active_rows[0] + 1] * g[0:1, :]
        for t in range(1, ntier):
            a = active_rows[t]
            acc = acc + own_op[:, a : a + 1] * g[t : t + 1, :]
        lifts.append(acc)

    wait_for(out, r_o)
    for j in range(width // C):
        for r in range(rows):
            out[r, :, j * C : (j + 1) * C] += lifts[j]

    for copies in (h_t, h_m, h_p, h_1):
        halo_sent(copies)
    sent = pl.ds(0, nwin - 1)
    wait_for(res.at[sent], s_t)
    wait_for(res.at[sent], s_m)
    wait_for(res.at[sent], s_o)
    wait_for(pk_out.at[sent, 0], s_pk)
    all_but_one(p1g, s_p1g)
    all_but_one(p2g, s_p2g)
    all_but_one(p1z, s_p1z)
    all_but_one(p2z, s_p2z)


def solution(mesh):
    ntier, ntile = mesh.shape["tier"], mesh.shape["tile"]

    def shards(temp, mats, rates, labels, stat, fac, op):
        rows, lev, width = temp.shape
        nblk = stat.shape[1]
        pad = -(-nblk // 128) * 128
        group = width // (ntier * C)
        levels, grows, ngrp, nwin = lev * ntier, rows * group, ntile // group, width // C
        f32, i32 = jnp.float32, jnp.int32
        vm = lambda shape, dtype=f32: pltpu.VMEM(shape, dtype)
        dma = pltpu.SemaphoreType.DMA
        vmem = pl.BlockSpec(memory_space=pltpu.VMEM)
        field = (grows, levels, C)
        return pl.pallas_call(
            functools.partial(kernel, ntier, ntile, nblk, group),
            out_shape=(
                jax.ShapeDtypeStruct(temp.shape, f32),
                jax.ShapeDtypeStruct((1, nblk), f32),
            ),
            in_specs=[pl.BlockSpec(memory_space=pltpu.HBM)] * 7,
            out_specs=(vmem, vmem),
            scratch_shapes=[
                vm(temp.shape), vm(mats.shape, i32), vm(rates.shape),
                pltpu.SMEM(labels.shape, i32), vm(stat.shape), vm(fac.shape), vm(op.shape),
                dma((7,)),
                vm(field), vm(field, i32), vm((2, levels, C)), vm((2, levels, C), i32), vm((2, levels, C)),
                vm((nwin, lev // 8, 8, C)), vm((group, ntier, 8, C)), vm((2, ntier, 8, C)),
                vm((grows + 1, levels, C)), vm(field), vm(field), vm((levels, (grows + 1) * C)),
                vm(field), vm((levels, C)), vm(field),
                vm((nwin, 8, pad)), vm((ngrp, 8, pad)), vm((nwin, 8, pad)), vm((ngrp, 8, pad)),
                dma, dma, dma, dma,
                dma((group,)), dma((group,)), dma, dma, dma, dma,
                dma((4, 2)), dma((4, 2)),
                dma, dma, dma, dma, dma, dma, dma, dma,
            ],
            compiler_params=pltpu.CompilerParams(
                collective_id=0, has_side_effects=True, vmem_limit_bytes=62 * 1024 * 1024
            ),
        )(temp, mats, rates, labels, stat, fac, op)

    return jax.shard_map(
        shards,
        mesh=mesh,
        in_specs=(P("tile", "tier", None), P("tile", "tier", None), P(), P("tile", None), P(), P(), P()),
        out_specs=(P("tile", "tier", None), P("tier", None)),
        check_vma=False,
    )
```

```python
import functools

import jax
import jax.numpy as jnp
from jax import lax
from jax.experimental import pallas as pl
from jax.experimental.pallas import tpu as pltpu
from jax.sharding import PartitionSpec as P

C = 128
RATE = 0.12
SOURCE_GAIN = 0.02
MESH = pl.DeviceIdType.MESH


def solve(op, x):
    return jnp.dot(op, x, precision=lax.Precision.HIGHEST, preferred_element_type=jnp.float32)


def roll(x, shift):
    return pltpu.roll(x, shift % C, x.ndim - 1) if shift % C else x


def kernel(
    ntier, ntile, nblk, group,
    t_hbm, m_hbm, rates_hbm, labels_hbm, stat_hbm, fac_hbm, a_hbm,
    out, pw_out, lift_out,
    t_in, m_in, rates, labels, stat, fac, a_in, s_in,
    col_t, col_m, halo_t, halo_m, halo_1,
    pk_out, pk, halo_p,
    cx, cy, ce, mv, t1, t1c, res,
    p1g, p1z, p2g, p2z,
    s_t, s_m, s_pk, s_o,
    r_et, r_em, r_rt, r_rm, r_pk, r_o,
    s_h, r_h,
    s_p1g, r_p1g, s_p1z, r_p1z, s_p2g, r_p2g, s_p2z, r_p2z,
):
    tier = lax.axis_index("tier")
    tile = lax.axis_index("tile")
    rows, lev, width = t_in.shape
    levels = lev * ntier
    nmat = rates.shape[1]
    ngrp = ntile // group
    grows = rows * group
    sub = lax.rem(tile, group)
    base = tile - sub
    place = tile // group
    own = tier * group + sub
    nwin = ntier * group
    active_rows = [t * lev for t in range(ntier)]

    loads = [
        pltpu.make_async_copy(src, dst, s_in.at[i])
        for i, (src, dst) in enumerate(
            ((t_hbm, t_in), (m_hbm, m_in), (labels_hbm, labels), (rates_hbm, rates),
             (stat_hbm, stat), (fac_hbm, fac), (a_hbm, a_in))
        )
    ]
    for load in loads:
        load.start()

    peers = []
    for a in range(ntier):
        for b in range(group):
            t2 = lax.rem(tier + a, ntier)
            s2 = lax.rem(sub + b, group)
            peers.append((a == 0 and b == 0, t2, s2))

    def there(t2, s2):
        return {"tier": t2, "tile": base + s2}

    barrier = pltpu.get_barrier_semaphore()
    for mine, t2, s2 in peers:
        if not mine:
            pl.semaphore_signal(barrier, inc=1, device_id=there(t2, s2), device_id_type=MESH)

    def across(k):
        return {"tile": lax.rem(tile + k * group, ntile)}

    def greet(k, carry):
        pl.semaphore_signal(barrier, inc=1, device_id=across(k), device_id_type=MESH)
        return carry

    lax.fori_loop(1, ngrp, greet, 0)

    def cols(w):
        return pl.ds(pl.multiple_of(w * C, C), C)

    def levs(t):
        return pl.ds(pl.multiple_of(t * lev, 8), lev)

    lane = lax.broadcasted_iota(jnp.int32, (1, C), 1)
    blk = lax.broadcasted_iota(jnp.int32, (1, nblk), 1)

    for load in loads:
        load.wait()

    sums = jnp.zeros((1, nblk), jnp.float32)
    areas = jnp.zeros((1, nblk), jnp.float32)
    names = jnp.zeros((1, C), jnp.float32)
    active = t_in[0, 0:1, :]
    for r in range(1, rows):
        active = active + t_in[r, 0:1, :]
    for j in range(width // C):
        part = jnp.sum(active[:, j * C : (j + 1) * C], axis=1, keepdims=True)
        hit = blk == labels[0, j]
        sums = sums + jnp.where(hit, part, 0.0)
        areas = areas + jnp.where(hit, float(rows * C), 0.0)
        names = jnp.where(lane == j, labels[0, j].astype(jnp.float32), names)
    p1g[own] = jnp.zeros(p1g.shape[1:], jnp.float32)
    p1g[own, 0:1, 0:nblk] = sums
    p1g[own, 1:2, 0:nblk] = areas
    p1g[own, 2:3, 0:C] = names

    pl.semaphore_wait(barrier, nwin - 1 + ngrp - 1)

    def group_send(buf, s_sem, r_sem):
        for mine, t2, s2 in peers:
            if not mine:
                pltpu.make_async_remote_copy(
                    src_ref=buf.at[own], dst_ref=buf.at[own], send_sem=s_sem, recv_sem=r_sem,
                    device_id=there(t2, s2), device_id_type=MESH,
                ).start()

    def across_send(buf, s_sem, r_sem):
        def send(k, carry):
            pltpu.make_async_remote_copy(
                src_ref=buf.at[0], dst_ref=buf.at[k], send_sem=s_sem, recv_sem=r_sem,
                device_id=across(k), device_id_type=MESH,
            ).start()
            return carry

        lax.fori_loop(1, ngrp, send, 0)

    def wait_for(ref, sem):
        pltpu.make_async_copy(ref, ref, sem).wait()

    def all_but_one(buf, sem):
        wait_for(buf.at[pl.ds(1, buf.shape[0] - 1)], sem)

    def total(buf):
        return lax.fori_loop(1, ngrp, lambda k, acc: acc + buf[k], buf[0])

    group_send(p1g, s_p1g, r_p1g)

    def spread(src, dst, row, to, count, s_sem, r_sem):
        for mine, t2, s2 in peers:
            src_ref = src.at[pl.ds(row, count), :, cols(t2 * group + s2)]
            dst_ref = dst.at[pl.ds(to, count), levs(tier), :]
            if mine:
                pltpu.make_async_copy(src_ref, dst_ref, r_sem).start()
            else:
                pltpu.make_async_remote_copy(
                    src_ref=src_ref, dst_ref=dst_ref, send_sem=s_sem, recv_sem=r_sem,
                    device_id=there(t2, s2), device_id_type=MESH,
                ).start()

    edge = lax.select(sub == 0, 0, rows - 1)
    rest = lax.select(sub == 0, 1, 0)
    spread(t_hbm, col_t, edge, sub * rows + edge, 1, s_t, r_et.at[sub])
    spread(m_hbm, col_m, edge, sub * rows + edge, 1, s_m, r_em.at[sub])

    quad = lane >> 2
    for w in range(nwin):
        low = max(w - 1, 0) * C
        high = min(w + 1, nwin - 1) * C
        for g in range(lev // 8):
            ls = slice(8 * g, 8 * g + 8)
            acc = None
            for q, src in ((0, t_in), (rows, m_in)):
                for r in range(rows):
                    both = jnp.where(
                        lane >= 64, src[r, ls, low : low + C], src[r, ls, high : high + C]
                    )
                    if q:
                        both = both.astype(jnp.float32)
                    put = roll(both, 32 * g + 4 * (q + r) + 2)
                    acc = put if acc is None else jnp.where(quad == 8 * g + q + r, put, acc)
            pk_out[w, g] = acc

    def fold(w):
        total_p = None
        for g in range(lev // 8):
            piece = pk_out[w, g]
            keep = (lane >= 32 * g) & (lane < 32 * g + 32)
            total_p = jnp.where(keep, piece, 0.0) if total_p is None else jnp.where(keep, piece, total_p)
        return total_p

    for w in range(nwin):
        pk_out[w, 0] = fold(w)

    for mine, t2, s2 in peers:
        src_ref, dst_ref = pk_out.at[t2 * group + s2, 0], pk.at[sub, tier]
        if mine:
            pltpu.make_async_copy(src_ref, dst_ref, r_pk).start()
        else:
            pltpu.make_async_remote_copy(
                src_ref=src_ref, dst_ref=dst_ref, send_sem=s_pk, recv_sem=r_pk,
                device_id=there(t2, s2), device_id_type=MESH,
            ).start()
    spread(m_hbm, col_m, rest, sub * rows + rest, rows - 1, s_m, r_rm)
    spread(t_hbm, col_t, rest, sub * rows + rest, rows - 1, s_t, r_rt)

    has_low = place > 0
    has_high = place < ngrp - 1

    @pl.when(jnp.logical_not(has_low))
    def _():
        for ref in (halo_t, halo_m, halo_p, halo_1):
            ref[0] = jnp.zeros(ref.shape[1:], ref.dtype)

    @pl.when(jnp.logical_not(has_high))
    def _():
        for ref in (halo_t, halo_m, halo_p, halo_1):
            ref[1] = jnp.zeros(ref.shape[1:], ref.dtype)

    def halo(low_src, high_src, dst, which):
        down = pltpu.make_async_remote_copy(
            src_ref=low_src, dst_ref=dst.at[1],
            send_sem=s_h.at[which, 0], recv_sem=r_h.at[which, 1],
            device_id={"tile": lax.max(tile - group, sub)}, device_id_type=MESH,
        )
        up = pltpu.make_async_remote_copy(
            src_ref=high_src, dst_ref=dst.at[0],
            send_sem=s_h.at[which, 1], recv_sem=r_h.at[which, 0],
            device_id={"tile": lax.min(tile + group, ntile - group + sub)}, device_id_type=MESH,
        )
        return down, up

    def halo_recv(copies):
        pl.when(has_low)(lambda: copies[1].wait_recv())
        pl.when(has_high)(lambda: copies[0].wait_recv())

    def halo_sent(copies):
        pl.when(has_low)(lambda: copies[0].wait_send())
        pl.when(has_high)(lambda: copies[1].wait_send())

    h_t = halo(col_t.at[0], col_t.at[grows - 1], halo_t, 0)
    h_m = halo(col_m.at[0], col_m.at[grows - 1], halo_m, 1)
    h_p = halo(pk.at[0], pk.at[group - 1], halo_p, 2)
    h_1 = halo(t1.at[0], t1.at[grows - 1], halo_1, 3)

    all_but_one(p1g, r_p1g)
    p1z[0] = jnp.zeros(p1z.shape[1:], jnp.float32)
    for t in range(ntier):
        acc = p1g[t * group, 0:1, :]
        for s in range(1, group):
            acc = acc + p1g[t * group + s, 0:1, :]
        p1z[0, t : t + 1, :] = acc
    acc = p1g[0, 1:2, :]
    for s in range(1, group):
        acc = acc + p1g[s, 1:2, :]
    p1z[0, ntier : ntier + 1, :] = acc
    across_send(p1z, s_p1z, r_p1z)

    for s, row in ((0, 0), (group - 1, grows - 1)):
        wait_for(col_t.at[row], r_et.at[s])
        wait_for(col_m.at[row], r_em.at[s])
    pl.when(has_low)(lambda: (h_m[0].start(), h_t[0].start()) and None)
    pl.when(has_high)(lambda: (h_m[1].start(), h_t[1].start()) and None)
    wait_for(pk, r_pk)
    pl.when(has_low)(lambda: h_p[0].start())
    pl.when(has_high)(lambda: h_p[1].start())

    inverse = 1.0 / ((2.0 * RATE) * rates[...])
    table = [
        [jnp.broadcast_to(inverse[a : a + 1, m : m + 1], (1, C)) for m in range(nmat)]
        for a in range(2)
    ]

    def lookup(codes, axes):
        outs = [jnp.broadcast_to(table[a][0], codes.shape) for a in axes]
        for m in range(1, nmat):
            hit = codes == m
            outs = [jnp.where(hit, table[a][m], o) for a, o in zip(axes, outs)]
        return outs

    def unpack(low, high, shift_low, shift_high, split):
        pieces = []
        for t in range(ntier):
            for g in range(lev // 8):
                a = roll(low(t), shift_low - 32 * g)
                if high is not None:
                    a = jnp.where(lane < split, a, roll(high(t), shift_high - 32 * g))
                pieces.append(a)
        return jnp.concatenate(pieces, axis=0)

    def swap(x):
        return jnp.where((lane & 3) == 1, roll(x, -1), roll(x, 1))

    half = 4 * rows
    out_t = unpack(lambda t: pk[0, t], lambda t: pk[1, t], 0, half, half)
    out_m = unpack(lambda t: pk[0, t], lambda t: pk[1, t], -half, 0, half)
    ixc, iyc = lookup(out_m, (0, 1))
    pos_low = (lane & 3) == 1

    wait_for(col_m.at[pl.ds(1, grows - 2)], r_rm)
    before = None
    inner = jnp.ones((levels, C), jnp.float32)
    for r in range(grows):
        ix, iy = lookup(col_m[r], (0, 1))
        cy[r] = 1.0 / (iy + roll(iy, -1))
        inner = jnp.where((lane >> 2) == r, roll(iy, 4 * r + 2), inner)
        if r == 0:
            first = ix
        else:
            cx[r] = 1.0 / (before + ix)
        before = ix
    last = before

    there_is = jnp.where(pos_low, jnp.where(own > 0, 1.0, 0.0), jnp.where(own < nwin - 1, 1.0, 0.0))
    c_in = there_is / (iyc + swap(inner))
    c_far = 1.0 / (iyc + jnp.where(pos_low, roll(iyc, 1), roll(iyc, -1)))
    spun = swap(c_in)
    for r in range(grows):
        ce[r] = roll(spun, -(4 * r + 2))
        cy[r] = jnp.where(lane == C - 1, ce[r], cy[r])

    halo_recv(h_m)
    halo_recv(h_p)
    (ix,) = lookup(halo_m[0], (0,))
    cx[0] = jnp.where(has_low, 1.0 / (ix + first), 0.0)
    (ix,) = lookup(halo_m[1], (0,))
    cx[grows] = jnp.where(has_high, 1.0 / (ix + last), 0.0)

    end = 4 * (rows - 1)
    up_t = unpack(lambda t: halo_p[0, t], None, -end, 0, 0)
    up_m = unpack(lambda t: halo_p[0, t], None, -end - half, 0, 0)
    dn_t = unpack(lambda t: halo_p[1, t], None, 4 * (grows - 1), 0, 0)
    dn_m = unpack(lambda t: halo_p[1, t], None, 4 * (grows - 1) - half, 0, 0)
    (up_ix,) = lookup(up_m, (0,))
    (dn_ix,) = lookup(dn_m, (0,))
    at_top = lane < 4
    at_bottom = lane >= 4 * (grows - 1)
    up_c = 1.0 / (ixc + jnp.where(at_top, up_ix, roll(ixc, 4)))
    up_c = jnp.where(jnp.logical_and(at_top, jnp.logical_not(has_low)), 0.0, up_c)
    dn_c = 1.0 / (ixc + jnp.where(at_bottom, dn_ix, roll(ixc, -4)))
    dn_c = jnp.where(jnp.logical_and(at_bottom, jnp.logical_not(has_high)), 0.0, dn_c)
    part = (
        out_t
        + up_c * (jnp.where(at_top, up_t, roll(out_t, 4)) - out_t)
        + dn_c * (jnp.where(at_bottom, dn_t, roll(out_t, -4)) - out_t)
        + c_far * (jnp.where(pos_low, roll(out_t, 1), roll(out_t, -1)) - out_t)
    )

    op = a_in[...]
    op_active = [op[:, a : a + 1] for a in active_rows]

    all_but_one(p1z, r_p1z)
    whole = total(p1z)
    count = whole[ntier : ntier + 1, 0:nblk]
    power = stat[...] * jnp.exp(fac[...] * whole[0:ntier, 0:nblk] / count)

    def label_of(s, w):
        return jnp.sum(jnp.where(lane == w, p1g[s, 2:3, 0:C], 0.0), axis=1, keepdims=True)

    blkf = blk.astype(jnp.float32)

    def gain_of(pw, label):
        return SOURCE_GAIN * jnp.sum(jnp.where(blkf == label, pw, 0.0), axis=1, keepdims=True)

    own_labels = [label_of(s, own) for s in range(group)]
    gains = [gain_of(power, label) for label in own_labels]
    lift = []
    for s in range(group):
        acc = op_active[0] * gains[s][0:1, :]
        for t in range(1, ntier):
            acc = acc + op_active[t] * gains[s][t : t + 1, :]
        lift.append(acc)
    side = jnp.zeros((ntier, C), jnp.float32)
    for s in range(group):
        gl = gain_of(power, label_of(s, own - 1))
        gr = gain_of(power, label_of(s, own + 1))
        side = jnp.where(lane // half == s, jnp.where(pos_low, gl, gr), side)
    lift_c = op_active[0] * side[0:1, :]
    for t in range(1, ntier):
        lift_c = lift_c + op_active[t] * side[t : t + 1, :]

    def lateral(field, outside, r, above, below):
        here = field[r]
        edge_in = roll(outside, -(4 * r + 2))
        beside = jnp.where(lane == C - 1, edge_in, roll(here, -1))
        flux = cy[r] * (beside - here)
        left = jnp.where(lane == 0, ce[r] * (here - edge_in), roll(flux, 1))
        moved = here + (flux - left)
        return moved + cx[r + 1] * (below - here) - cx[r] * (here - above)

    halo_recv(h_t)
    wait_for(col_t.at[pl.ds(1, grows - 2)], r_rt)
    spun = swap(out_t)
    inner = out_t
    for r in range(grows):
        above = halo_t[0] if r == 0 else col_t[r - 1]
        below = halo_t[1] if r == grows - 1 else col_t[r + 1]
        mv[:, r * C : (r + 1) * C] = lateral(col_t, spun, r, above, below)
        inner = jnp.where((lane >> 2) == r, roll(col_t[r], 4 * r + 2), inner)
    mv[:, grows * C : (grows + 1) * C] = part + c_in * (swap(inner) - out_t)

    order = [0, grows - 1] + list(range(1, grows - 1))
    for r in order:
        t1[r] = solve(op, mv[:, r * C : (r + 1) * C]) + lift[r // rows]
        if r == grows - 1:
            pl.when(has_low)(lambda: h_1[0].start())
            pl.when(has_high)(lambda: h_1[1].start())
    t1c = solve(op, mv[:, grows * C : (grows + 1) * C]) + lift_c

    p2g[own] = jnp.zeros(p2g.shape[1:], jnp.float32)
    sums = jnp.zeros((ntier, nblk), jnp.float32)
    for s in range(group):
        acc = []
        for a in active_rows:
            v = t1[s * rows, a : a + 1, :]
            for r in range(1, rows):
                v = v + t1[s * rows + r, a : a + 1, :]
            acc.append(v)
        acc = jnp.sum(jnp.concatenate(acc, axis=0), axis=1, keepdims=True)
        sums = sums + jnp.where(blkf == own_labels[s], acc, 0.0)
    p2g[own, 0:ntier, 0:nblk] = sums
    group_send(p2g, s_p2g, r_p2g)

    def send_rows(s, first_row, count):
        for t in range(ntier):
            for_me = jnp.logical_and(tier == t, sub == s)
            src_ref = res.at[pl.ds(s * rows + first_row, count), pl.ds(t * lev, lev), :]
            dst_ref = out.at[pl.ds(first_row, count), :, cols(own)]

            @pl.when(for_me)
            def _():
                pltpu.make_async_copy(src_ref, dst_ref, r_o).start()

            @pl.when(jnp.logical_not(for_me))
            def _():
                pltpu.make_async_remote_copy(
                    src_ref=src_ref, dst_ref=dst_ref, send_sem=s_o, recv_sem=r_o,
                    device_id=there(t, s), device_id_type=MESH,
                ).start()

    spun = swap(t1c)

    def finish(r):
        above = halo_1[0] if r == 0 else t1[r - 1]
        below = halo_1[1] if r == grows - 1 else t1[r + 1]
        mv[:, r * C : (r + 1) * C] = lateral(t1, spun, r, above, below)
        res[r] = solve(op, mv[:, r * C : (r + 1) * C])

    for s in range(group):
        for r in range(s * rows + (s == 0), (s + 1) * rows - (s == group - 1)):
            finish(r)
        send_rows(s, int(s == 0), rows - 1)

    all_but_one(p2g, r_p2g)
    acc = p2g[0]
    for k in range(1, nwin):
        acc = acc + p2g[k]
    p2z[0] = acc
    across_send(p2z, s_p2z, r_p2z)

    halo_recv(h_1)
    for s, r in ((0, 0), (group - 1, grows - 1)):
        finish(r)
        send_rows(s, r - s * rows, 1)

    all_but_one(p2z, r_p2z)
    whole = total(p2z)
    power = stat[...] * jnp.exp(fac[...] * whole[0:ntier, 0:nblk] / count)
    mine = lax.broadcasted_iota(jnp.int32, (ntier, nblk), 0) == tier
    pw_out[...] = jnp.sum(jnp.where(mine, power, 0.0), axis=0, keepdims=True)
    own_op = a_in[levs(tier), :]
    for j in range(width // C):
        g = SOURCE_GAIN * jnp.sum(jnp.where(blk == labels[0, j], power, 0.0), axis=1, keepdims=True)
        acc = own_op[:, active_rows[0] : active_rows[0] + 1] * g[0:1, :]
        for t in range(1, ntier):
            a = active_rows[t]
            acc = acc + own_op[:, a : a + 1] * g[t : t + 1, :]
        lift_out[:, j * C : (j + 1) * C] = jnp.broadcast_to(acc, (lev, C))
    wait_for(out, r_o)

    for copies in (h_t, h_m, h_p, h_1):
        halo_sent(copies)
    sent = pl.ds(0, nwin - 1)
    wait_for(res.at[sent], s_t)
    wait_for(res.at[sent], s_m)
    wait_for(res.at[sent], s_o)
    wait_for(pk_out.at[sent, 0], s_pk)
    all_but_one(p1g, s_p1g)
    all_but_one(p2g, s_p2g)
    all_but_one(p1z, s_p1z)
    all_but_one(p2z, s_p2z)


def last(field, lift, power, out, power_out, done, sem):
    copies = []
    for r in range(field.shape[0]):
        done[r] = field[r] + lift[...]
        copies.append(pltpu.make_async_copy(done.at[r], out.at[r], sem.at[r]))
        copies[-1].start()
    copies.append(pltpu.make_async_copy(power, power_out, sem.at[field.shape[0]]))
    copies[-1].start()
    for copy in copies:
        copy.wait()


def solution(mesh):
    ntier, ntile = mesh.shape["tier"], mesh.shape["tile"]

    def shards(temp, mats, rates, labels, stat, fac, op):
        rows, lev, width = temp.shape
        nblk = stat.shape[1]
        pad = -(-nblk // 128) * 128
        group = width // (ntier * C)
        levels, grows, ngrp, nwin = lev * ntier, rows * group, ntile // group, width // C
        f32, i32 = jnp.float32, jnp.int32
        vm = lambda shape, dtype=f32: pltpu.VMEM(shape, dtype)
        dma = pltpu.SemaphoreType.DMA
        vmem = pl.BlockSpec(memory_space=pltpu.VMEM)
        block = (grows, levels, C)
        args = (temp, mats, rates, labels, stat, fac, op)
        args = [pltpu.with_memory_space_constraint(x, pltpu.HBM) for x in args]
        field, power, lift = pl.pallas_call(
            functools.partial(kernel, ntier, ntile, nblk, group),
            out_shape=(vm(temp.shape), vm((1, nblk)), vm((lev, width))),
            in_specs=[pl.BlockSpec(memory_space=pltpu.HBM)] * 7,
            out_specs=(vmem, vmem, vmem),
            scratch_shapes=[
                vm(temp.shape), vm(mats.shape, i32), vm(rates.shape),
                pltpu.SMEM(labels.shape, i32), vm(stat.shape), vm(fac.shape), vm(op.shape),
                dma((7,)),
                vm(block), vm(block, i32), vm((2, levels, C)), vm((2, levels, C), i32), vm((2, levels, C)),
                vm((nwin, lev // 8, 8, C)), vm((group, ntier, 8, C)), vm((2, ntier, 8, C)),
                vm((grows + 1, levels, C)), vm(block), vm(block), vm((levels, (grows + 1) * C)),
                vm(block), vm((levels, C)), vm(block),
                vm((nwin, 8, pad)), vm((ngrp, 8, pad)), vm((nwin, 8, pad)), vm((ngrp, 8, pad)),
                dma, dma, dma, dma,
                dma((group,)), dma((group,)), dma, dma, dma, dma,
                dma((4, 2)), dma((4, 2)),
                dma, dma, dma, dma, dma, dma, dma, dma,
            ],
            compiler_params=pltpu.CompilerParams(
                collective_id=0, has_side_effects=True, vmem_limit_bytes=48 * 1024 * 1024
            ),
        )(*args)
        anywhere = pl.BlockSpec(memory_space=pltpu.HBM)
        return pl.pallas_call(
            last,
            out_shape=(
                jax.ShapeDtypeStruct(temp.shape, f32),
                jax.ShapeDtypeStruct((1, nblk), f32),
            ),
            in_specs=[vmem] * 3,
            out_specs=(anywhere, anywhere),
            scratch_shapes=[vm(temp.shape), dma((rows + 1,))],
            compiler_params=pltpu.CompilerParams(vmem_limit_bytes=4 * 1024 * 1024),
        )(field, lift, power)

    return jax.shard_map(
        shards,
        mesh=mesh,
        in_specs=(P("tile", "tier", None), P("tile", "tier", None), P(), P("tile", None), P(), P(), P()),
        out_specs=(P("tile", "tier", None), P("tier", None)),
        check_vma=False,
    )
```

```python
import functools

import jax
import jax.numpy as jnp
from jax import lax
from jax.experimental import pallas as pl
from jax.experimental.pallas import tpu as pltpu
from jax.sharding import PartitionSpec as P

C = 128
RATE = 0.12
SOURCE_GAIN = 0.02
MESH = pl.DeviceIdType.MESH


def split(x):
    high = x.astype(jnp.bfloat16)
    return high, (x - high.astype(jnp.float32)).astype(jnp.bfloat16)


def solve(op, x):
    high, low = split(x)
    n = op.shape[0] // 2
    both = jnp.dot(op, high, preferred_element_type=jnp.float32)
    more = jnp.dot(op[:n], low, preferred_element_type=jnp.float32)
    return both[:n] + (both[n:] + more)


def roll(x, shift):
    return pltpu.roll(x, shift % C, x.ndim - 1) if shift % C else x


def kernel(
    ntier, ntile, nblk, group,
    t_hbm, m_hbm, rates_hbm, labels_hbm, stat_hbm, fac_hbm, a_hbm,
    out, pw_out, lift_out,
    t_in, m_in, rates, labels, stat, fac, a_in, s_in,
    col_t, col_m, halo_t, halo_m, halo_1,
    pk_out, pk, halo_p,
    cx, cy, ce, mv, t1, t1c, res,
    p1g, p1z, p2g, p2z,
    s_t, s_m, s_pk, s_o,
    r_et, r_em, r_at, r_am, r_it, r_rt, r_rm, r_pk, r_o,
    s_h, r_h,
    s_p1g, r_p1g, s_p1z, r_p1z, s_p2g, r_p2g, s_p2z, r_p2z, entered,
):
    tier = lax.axis_index("tier")
    tile = lax.axis_index("tile")
    rows, lev, width = t_in.shape
    levels = lev * ntier
    nmat = rates.shape[1]
    ngrp = ntile // group
    grows = rows * group
    sub = lax.rem(tile, group)
    base = tile - sub
    place = tile // group
    own = tier * group + sub
    nwin = ntier * group
    active_rows = [t * lev for t in range(ntier)]

    loads = [
        pltpu.make_async_copy(src, dst, s_in.at[i])
        for i, (src, dst) in enumerate(
            ((t_hbm, t_in), (m_hbm, m_in), (labels_hbm, labels), (rates_hbm, rates),
             (stat_hbm, stat), (fac_hbm, fac), (a_hbm, a_in))
        )
    ]
    for load in loads:
        load.start()

    peers = []
    for a in range(ntier):
        for b in range(group):
            t2 = lax.rem(tier + a, ntier)
            s2 = lax.rem(sub + b, group)
            peers.append((a == 0 and b == 0, t2, s2))

    def there(t2, s2):
        return {"tier": t2, "tile": base + s2}

    barrier = pltpu.get_barrier_semaphore()
    for mine, t2, s2 in peers:
        if not mine:
            pl.semaphore_signal(barrier, inc=1, device_id=there(t2, s2), device_id_type=MESH)

    def across(k):
        return {"tile": lax.rem(tile + k * group, ntile)}

    def greet(sem, low, high):
        def one(k, carry):
            pl.semaphore_signal(
                sem, inc=1, device_id={"tile": k * group + sub}, device_id_type=MESH
            )
            return carry

        lax.fori_loop(low, high, one, 0)

    greet(barrier, place + 1, ngrp)

    def cols(w):
        return pl.ds(pl.multiple_of(w * C, C), C)

    def levs(t):
        return pl.ds(pl.multiple_of(t * lev, 8), lev)

    lane = lax.broadcasted_iota(jnp.int32, (1, C), 1)
    blk = lax.broadcasted_iota(jnp.int32, (1, nblk), 1)

    for load in loads:
        load.wait()

    sums = jnp.zeros((1, nblk), jnp.float32)
    areas = jnp.zeros((1, nblk), jnp.float32)
    names = jnp.zeros((1, C), jnp.float32)
    active = t_in[0, 0:1, :]
    for r in range(1, rows):
        active = active + t_in[r, 0:1, :]
    for j in range(width // C):
        part = jnp.sum(active[:, j * C : (j + 1) * C], axis=1, keepdims=True)
        hit = blk == labels[0, j]
        sums = sums + jnp.where(hit, part, 0.0)
        areas = areas + jnp.where(hit, float(rows * C), 0.0)
        names = jnp.where(lane == j, labels[0, j].astype(jnp.float32), names)
    p1g[own] = jnp.zeros(p1g.shape[1:], jnp.float32)
    p1g[own, 0:1, 0:nblk] = sums
    p1g[own, 1:2, 0:nblk] = areas
    p1g[own, 2:3, 0:C] = names

    pl.semaphore_wait(barrier, nwin - 1 + place)
    greet(entered, 0, place)

    def group_send(buf, s_sem, r_sem):
        for mine, t2, s2 in peers:
            if not mine:
                pltpu.make_async_remote_copy(
                    src_ref=buf.at[own], dst_ref=buf.at[own], send_sem=s_sem, recv_sem=r_sem,
                    device_id=there(t2, s2), device_id_type=MESH,
                ).start()

    def across_send(buf, s_sem, r_sem):
        def send(k, carry):
            pltpu.make_async_remote_copy(
                src_ref=buf.at[0], dst_ref=buf.at[k], send_sem=s_sem, recv_sem=r_sem,
                device_id=across(k), device_id_type=MESH,
            ).start()
            return carry

        lax.fori_loop(1, ngrp, send, 0)

    def wait_for(ref, sem):
        pltpu.make_async_copy(ref, ref, sem).wait()

    def all_but_one(buf, sem):
        wait_for(buf.at[pl.ds(1, buf.shape[0] - 1)], sem)

    def total(buf):
        return lax.fori_loop(1, ngrp, lambda k, acc: acc + buf[k], buf[0])

    group_send(p1g, s_p1g, r_p1g)

    def spread(src, dst, row, to, count, s_sem, r_sem):
        for mine, t2, s2 in peers:
            src_ref = src.at[pl.ds(row, count), :, cols(t2 * group + s2)]
            dst_ref = dst.at[pl.ds(to, count), levs(tier), :]
            if mine:
                pltpu.make_async_copy(src_ref, dst_ref, r_sem).start()
            else:
                pltpu.make_async_remote_copy(
                    src_ref=src_ref, dst_ref=dst_ref, send_sem=s_sem, recv_sem=r_sem,
                    device_id=there(t2, s2), device_id_type=MESH,
                ).start()

    edge = lax.select(sub == 0, 0, rows - 1)
    beside = lax.select(sub == 0, 1, rows - 2)
    rest = lax.select(sub == 0, 2, 0)
    inmost = lax.select(sub == 0, rows - 1, 0)
    other = lax.select(sub == 0, rows - 2, 1)
    spread(t_hbm, col_t, edge, sub * rows + edge, 1, s_t, r_et.at[sub])
    spread(m_hbm, col_m, edge, sub * rows + edge, 1, s_m, r_em.at[sub])

    quad = lane >> 2
    for w in range(nwin):
        low = max(w - 1, 0) * C
        high = min(w + 1, nwin - 1) * C
        first = second = None
        for g in range(lev // 8):
            ls = slice(8 * g, 8 * g + 8)
            for q, src in ((0, t_in), (rows, m_in)):
                for r in range(rows):
                    both = jnp.where(
                        lane >= 64, src[r, ls, low : low + C], src[r, ls, high : high + C]
                    )
                    if q:
                        both = both.astype(jnp.float32)
                    put = roll(both, 32 * g + 4 * (q + r) + 2)
                    first = put if first is None else jnp.where(quad == 8 * g + q + r, put, first)
            whole = None
            for r in range(rows):
                block = t_in[r, ls, w * C : (w + 1) * C]
                whole = block if whole is None else whole + block
                put = roll(block, 32 * g + 4 * r + 2)
                second = put if second is None else jnp.where(quad == 8 * g + r, put, second)
            whole = jnp.sum(whole, axis=1, keepdims=True)
            second = jnp.where(lane == 32 * g + 3, whole, second)
        pk_out[w, 0] = first
        pk_out[w, 1] = second

    for mine, t2, s2 in peers:
        src_ref, dst_ref = pk_out.at[t2 * group + s2], pk.at[sub, tier]
        if mine:
            pltpu.make_async_copy(src_ref, dst_ref, r_pk).start()
        else:
            pltpu.make_async_remote_copy(
                src_ref=src_ref, dst_ref=dst_ref, send_sem=s_pk, recv_sem=r_pk,
                device_id=there(t2, s2), device_id_type=MESH,
            ).start()
    spread(m_hbm, col_m, beside, sub * rows + beside, 1, s_m, r_am.at[sub])
    spread(t_hbm, col_t, beside, sub * rows + beside, 1, s_t, r_at.at[sub])
    spread(m_hbm, col_m, rest, sub * rows + rest, rows - 2, s_m, r_rm)
    spread(t_hbm, col_t, inmost, sub * rows + inmost, 1, s_t, r_it)
    spread(t_hbm, col_t, other, sub * rows + other, 1, s_t, r_rt.at[sub])

    has_low = place > 0
    has_high = place < ngrp - 1

    @pl.when(jnp.logical_not(has_low))
    def _():
        for ref in (halo_t, halo_m, halo_p, halo_1):
            ref[0] = jnp.zeros(ref.shape[1:], ref.dtype)

    @pl.when(jnp.logical_not(has_high))
    def _():
        for ref in (halo_t, halo_m, halo_p, halo_1):
            ref[1] = jnp.zeros(ref.shape[1:], ref.dtype)

    def halo(low_src, high_src, dst, which):
        down = pltpu.make_async_remote_copy(
            src_ref=low_src, dst_ref=dst.at[1],
            send_sem=s_h.at[which, 0], recv_sem=r_h.at[which, 1],
            device_id={"tile": lax.max(tile - group, sub)}, device_id_type=MESH,
        )
        up = pltpu.make_async_remote_copy(
            src_ref=high_src, dst_ref=dst.at[0],
            send_sem=s_h.at[which, 1], recv_sem=r_h.at[which, 0],
            device_id={"tile": lax.min(tile + group, ntile - group + sub)}, device_id_type=MESH,
        )
        return down, up

    def halo_recv(copies):
        pl.when(has_low)(lambda: copies[1].wait_recv())
        pl.when(has_high)(lambda: copies[0].wait_recv())

    def halo_sent(copies):
        pl.when(has_low)(lambda: copies[0].wait_send())
        pl.when(has_high)(lambda: copies[1].wait_send())

    h_t = halo(col_t.at[0], col_t.at[grows - 1], halo_t, 0)
    h_m = halo(col_m.at[0], col_m.at[grows - 1], halo_m, 1)
    h_p = halo(pk.at[0], pk.at[group - 1], halo_p, 2)
    h_1 = halo(t1.at[0], t1.at[grows - 1], halo_1, 3)

    all_but_one(p1g, r_p1g)
    p1z[0] = jnp.zeros(p1z.shape[1:], jnp.float32)
    for t in range(ntier):
        acc = p1g[t * group, 0:1, :]
        for s in range(1, group):
            acc = acc + p1g[t * group + s, 0:1, :]
        p1z[0, t : t + 1, :] = acc
    acc = p1g[0, 1:2, :]
    for s in range(1, group):
        acc = acc + p1g[s, 1:2, :]
    p1z[0, ntier : ntier + 1, :] = acc
    pl.when(has_high)(lambda: pl.semaphore_wait(entered, ngrp - 1 - place))
    across_send(p1z, s_p1z, r_p1z)

    for s, row in ((0, 0), (group - 1, grows - 1)):
        wait_for(col_t.at[row], r_et.at[s])
        wait_for(col_m.at[row], r_em.at[s])
    pl.when(has_low)(lambda: (h_m[0].start(), h_t[0].start()) and None)
    pl.when(has_high)(lambda: (h_m[1].start(), h_t[1].start()) and None)
    wait_for(pk, r_pk)
    pl.when(has_low)(lambda: h_p[0].start())
    pl.when(has_high)(lambda: h_p[1].start())

    inverse = 1.0 / ((2.0 * RATE) * rates[...])
    table = [
        [jnp.broadcast_to(inverse[a : a + 1, m : m + 1], (1, C)) for m in range(nmat)]
        for a in range(2)
    ]

    def lookup(codes, axes):
        outs = [jnp.broadcast_to(table[a][0], codes.shape) for a in axes]
        for m in range(1, nmat):
            hit = codes == m
            outs = [jnp.where(hit, table[a][m], o) for a, o in zip(axes, outs)]
        return outs

    def unpack(low, high, shift_low, shift_high, split):
        pieces = []
        for t in range(ntier):
            for g in range(lev // 8):
                a = roll(low(t), shift_low - 32 * g)
                if high is not None:
                    a = jnp.where(lane < split, a, roll(high(t), shift_high - 32 * g))
                pieces.append(a)
        return jnp.concatenate(pieces, axis=0)

    def swap(x):
        return jnp.where((lane & 3) == 1, roll(x, -1), roll(x, 1))

    half = 4 * rows
    out_t = unpack(lambda t: pk[0, t, 0], lambda t: pk[1, t, 0], 0, half, half)
    out_m = unpack(lambda t: pk[0, t, 0], lambda t: pk[1, t, 0], -half, 0, half)
    own_t = unpack(lambda t: pk[0, t, 1], lambda t: pk[1, t, 1], 0, half, half)
    ixc, iyc = lookup(out_m, (0, 1))
    pos_low = (lane & 3) == 1

    op_active = [a_in[:, a : a + 1] for a in active_rows]
    op = jnp.concatenate(split(a_in[...]), axis=0)

    all_but_one(p1z, r_p1z)
    whole = total(p1z)
    count = whole[ntier : ntier + 1, 0:nblk]
    power = stat[...] * jnp.exp(fac[...] * whole[0:ntier, 0:nblk] / count)

    def label_of(s, w):
        return jnp.sum(jnp.where(lane == w, p1g[s, 2:3, 0:C], 0.0), axis=1, keepdims=True)

    blkf = blk.astype(jnp.float32)

    def gain_of(pw, label):
        return SOURCE_GAIN * jnp.sum(jnp.where(blkf == label, pw, 0.0), axis=1, keepdims=True)

    own_labels = [label_of(s, own) for s in range(group)]
    gains = [gain_of(power, label) for label in own_labels]
    lift = []
    for s in range(group):
        acc = op_active[0] * gains[s][0:1, :]
        for t in range(1, ntier):
            acc = acc + op_active[t] * gains[s][t : t + 1, :]
        lift.append(acc)
    side = jnp.zeros((ntier, C), jnp.float32)
    for s in range(group):
        gl = gain_of(power, label_of(s, own - 1))
        gr = gain_of(power, label_of(s, own + 1))
        side = jnp.where(lane // half == s, jnp.where(pos_low, gl, gr), side)
    lift_c = op_active[0] * side[0:1, :]
    for t in range(1, ntier):
        lift_c = lift_c + op_active[t] * side[t : t + 1, :]

    kx = {}
    inner = {}
    far = jnp.ones((levels, C), jnp.float32)

    def conduct(r):
        kx[r], iy = lookup(col_m[r], (0, 1))
        cy[r] = 1.0 / (iy + roll(iy, -1))
        inner[r] = roll(iy, 4 * r + 2)
        for q in (r, r + 1):
            if q - 1 in kx and q in kx:
                cx[q] = 1.0 / (kx[q - 1] + kx[q])

    there_is = jnp.where(pos_low, jnp.where(own > 0, 1.0, 0.0), jnp.where(own < nwin - 1, 1.0, 0.0))

    def sideways(rs):
        at = jnp.ones((levels, C), jnp.float32)
        for r in rs:
            at = jnp.where((lane >> 2) == r, inner[r], at)
        c_in = there_is / (iyc + swap(at))
        spun = swap(c_in)
        for r in rs:
            ce[r] = roll(spun, -(4 * r + 2))
            cy[r] = jnp.where(lane == C - 1, ce[r], cy[r])
        return c_in

    c_far = 1.0 / (iyc + jnp.where(pos_low, roll(iyc, 1), roll(iyc, -1)))

    outer = [0, grows - 1]
    near = [1, grows - 2]
    middle = list(range(2, grows - 2))
    for s, row in ((0, 1), (group - 1, grows - 2)):
        wait_for(col_m.at[row], r_am.at[s])
    for r in outer + near:
        conduct(r)
    wait_for(col_m.at[pl.ds(2, grows - 4)], r_rm)
    for r in middle:
        conduct(r)
    first, last = kx[0], kx[grows - 1]
    c_in = sideways(range(grows))
    into_side = c_in * (swap(own_t) - out_t)

    halo_recv(h_m)
    halo_recv(h_p)
    (ix,) = lookup(halo_m[0], (0,))
    cx[0] = jnp.where(has_low, 1.0 / (ix + first), 0.0)
    (ix,) = lookup(halo_m[1], (0,))
    cx[grows] = jnp.where(has_high, 1.0 / (ix + last), 0.0)

    end = 4 * (rows - 1)
    up_t = unpack(lambda t: halo_p[0, t, 0], None, -end, 0, 0)
    up_m = unpack(lambda t: halo_p[0, t, 0], None, -end - half, 0, 0)
    dn_t = unpack(lambda t: halo_p[1, t, 0], None, 4 * (grows - 1), 0, 0)
    dn_m = unpack(lambda t: halo_p[1, t, 0], None, 4 * (grows - 1) - half, 0, 0)
    (up_ix,) = lookup(up_m, (0,))
    (dn_ix,) = lookup(dn_m, (0,))
    at_top = lane < 4
    at_bottom = lane >= 4 * (grows - 1)
    up_c = 1.0 / (ixc + jnp.where(at_top, up_ix, roll(ixc, 4)))
    up_c = jnp.where(jnp.logical_and(at_top, jnp.logical_not(has_low)), 0.0, up_c)
    dn_c = 1.0 / (ixc + jnp.where(at_bottom, dn_ix, roll(ixc, -4)))
    dn_c = jnp.where(jnp.logical_and(at_bottom, jnp.logical_not(has_high)), 0.0, dn_c)
    part = (
        out_t
        + up_c * (jnp.where(at_top, up_t, roll(out_t, 4)) - out_t)
        + dn_c * (jnp.where(at_bottom, dn_t, roll(out_t, -4)) - out_t)
        + into_side
        + c_far * (jnp.where(pos_low, roll(out_t, 1), roll(out_t, -1)) - out_t)
    )


    def lateral(field, outside, r, above, below):
        here = field[r]
        edge_in = roll(outside, -(4 * r + 2))
        beside = jnp.where(lane == C - 1, edge_in, roll(here, -1))
        flux = cy[r] * (beside - here)
        left = jnp.where(lane == 0, ce[r] * (here - edge_in), roll(flux, 1))
        moved = here + (flux - left)
        return moved + cx[r + 1] * (below - here) - cx[r] * (here - above)

    halo_recv(h_t)
    spun = swap(out_t)
    place_of = {r: i for i, r in enumerate(outer + [grows] + list(range(1, grows - 1)))}

    def at(r, n=1):
        return slice(place_of[r] * C, (place_of[r] + n) * C)

    def first_move(r):
        above = halo_t[0] if r == 0 else col_t[r - 1]
        below = halo_t[1] if r == grows - 1 else col_t[r + 1]
        mv[:, at(r)] = lateral(col_t, spun, r, above, below)

    for s, row in ((0, 1), (group - 1, grows - 2)):
        wait_for(col_t.at[row], r_at.at[s])
    for r in outer:
        first_move(r)
    mv[:, at(grows)] = part
    both = solve(op, mv[:, at(0, 3)])
    for i, r in enumerate(outer):
        t1[r] = both[:, i * C : (i + 1) * C] + lift[r // rows]
    t1c = both[:, 2 * C :] + lift_c
    pl.when(has_low)(lambda: h_1[0].start())
    pl.when(has_high)(lambda: h_1[1].start())

    wait_for(col_t.at[pl.ds(rows - 1, 2)], r_it)
    flows = [
        cx[0] * (halo_t[0] - col_t[0]),
        cx[rows] * (col_t[rows] - col_t[rows - 1]),
        cx[grows] * (halo_t[1] - col_t[grows - 1]),
    ]
    inflow = (flows[0] + flows[1], flows[2] - flows[1])
    side_lane = jnp.logical_or((lane & 3) == 1, (lane & 3) == 2)
    stock = []
    for s in range(group):
        mine = jnp.logical_and(lane // half == s, side_lane)
        stock.append(
            inflow[s]
            - jnp.where(mine, into_side, 0.0)
            + jnp.where(lane == s * half + 3, own_t, 0.0)
        )
    n_act = -(-ntier // 8) * 8
    act = jnp.concatenate(
        [a_in[a : a + 1, :] for a in active_rows]
        + [jnp.zeros((n_act - ntier, levels), jnp.float32)], axis=0
    )
    found = solve(jnp.concatenate(split(act), axis=0), jnp.concatenate(stock, axis=1))
    p2g[own] = jnp.zeros(p2g.shape[1:], jnp.float32)
    sums = jnp.zeros((ntier, nblk), jnp.float32)
    for s in range(group):
        acc = jnp.sum(found[0:ntier, s * C : (s + 1) * C], axis=1, keepdims=True)
        acc = acc + float(rows * C) * jnp.concatenate(
            [lift[s][a : a + 1, :] for a in active_rows], axis=0
        )
        sums = sums + jnp.where(blkf == own_labels[s], acc, 0.0)
    p2g[own, 0:ntier, 0:nblk] = sums
    group_send(p2g, s_p2g, r_p2g)

    for s, row in ((0, rows - 2), (group - 1, rows + 1)):
        wait_for(col_t.at[row], r_rt.at[s])
    for r in near + middle:
        first_move(r)
    most = solve(op, mv[:, at(1, grows - 2)])
    for r in range(1, grows - 1):
        t1[r] = most[:, (r - 1) * C : r * C] + lift[r // rows]

    def send_rows(s, first_row, count):
        for t in range(ntier):
            for_me = jnp.logical_and(tier == t, sub == s)
            src_ref = res.at[pl.ds(s * rows + first_row, count), pl.ds(t * lev, lev), :]
            dst_ref = out.at[pl.ds(first_row, count), :, cols(own)]

            @pl.when(for_me)
            def _():
                pltpu.make_async_copy(src_ref, dst_ref, r_o).start()

            @pl.when(jnp.logical_not(for_me))
            def _():
                pltpu.make_async_remote_copy(
                    src_ref=src_ref, dst_ref=dst_ref, send_sem=s_o, recv_sem=r_o,
                    device_id=there(t, s), device_id_type=MESH,
                ).start()

    spun = swap(t1c)

    def finish(rs):
        for r in rs:
            above = halo_1[0] if r == 0 else t1[r - 1]
            below = halo_1[1] if r == grows - 1 else t1[r + 1]
            mv[:, at(r)] = lateral(t1, spun, r, above, below)
        x = solve(op, mv[:, at(rs[0], len(rs))])
        for i, r in enumerate(rs):
            res[r] = x[:, i * C : (i + 1) * C]

    for s in range(group):
        finish(list(range(s * rows + (s == 0), (s + 1) * rows - (s == group - 1))))
        send_rows(s, int(s == 0), rows - 1)

    all_but_one(p2g, r_p2g)
    acc = p2g[0]
    for k in range(1, nwin):
        acc = acc + p2g[k]
    p2z[0] = acc
    across_send(p2z, s_p2z, r_p2z)

    halo_recv(h_1)
    finish(outer)
    for s, r in ((0, 0), (group - 1, grows - 1)):
        send_rows(s, r - s * rows, 1)

    all_but_one(p2z, r_p2z)
    whole = total(p2z)
    power = stat[...] * jnp.exp(fac[...] * whole[0:ntier, 0:nblk] / count)
    mine = lax.broadcasted_iota(jnp.int32, (ntier, nblk), 0) == tier
    pw_out[...] = jnp.sum(jnp.where(mine, power, 0.0), axis=0, keepdims=True)
    own_op = a_in[levs(tier), :]
    for j in range(width // C):
        g = SOURCE_GAIN * jnp.sum(jnp.where(blk == labels[0, j], power, 0.0), axis=1, keepdims=True)
        acc = own_op[:, active_rows[0] : active_rows[0] + 1] * g[0:1, :]
        for t in range(1, ntier):
            a = active_rows[t]
            acc = acc + own_op[:, a : a + 1] * g[t : t + 1, :]
        lift_out[:, j * C : (j + 1) * C] = jnp.broadcast_to(acc, (lev, C))
    wait_for(out, r_o)

    for copies in (h_t, h_m, h_p, h_1):
        halo_sent(copies)
    sent = pl.ds(0, nwin - 1)
    wait_for(res.at[sent], s_t)
    wait_for(res.at[sent], s_m)
    wait_for(res.at[sent], s_o)
    wait_for(pk_out.at[sent], s_pk)
    all_but_one(p1g, s_p1g)
    all_but_one(p1z, s_p1z)
    all_but_one(p2g, s_p2g)
    all_but_one(p2z, s_p2z)


def last(field, lift, power, out, power_out, done, sem):
    copies = []
    for r in range(field.shape[0]):
        done[r] = field[r] + lift[...]
        copies.append(pltpu.make_async_copy(done.at[r], out.at[r], sem.at[r]))
        copies[-1].start()
    copies.append(pltpu.make_async_copy(power, power_out, sem.at[field.shape[0]]))
    copies[-1].start()
    for copy in copies:
        copy.wait()


def solution(mesh):
    ntier, ntile = mesh.shape["tier"], mesh.shape["tile"]

    def shards(temp, mats, rates, labels, stat, fac, op):
        rows, lev, width = temp.shape
        nblk = stat.shape[1]
        pad = -(-nblk // 128) * 128
        group = width // (ntier * C)
        levels, grows, ngrp, nwin = lev * ntier, rows * group, ntile // group, width // C
        f32, i32 = jnp.float32, jnp.int32
        vm = lambda shape, dtype=f32: pltpu.VMEM(shape, dtype)
        dma = pltpu.SemaphoreType.DMA
        vmem = pl.BlockSpec(memory_space=pltpu.VMEM)
        block = (grows, levels, C)
        args = (temp, mats, rates, labels, stat, fac, op)
        args = [pltpu.with_memory_space_constraint(x, pltpu.HBM) for x in args]
        field, power, lift = pl.pallas_call(
            functools.partial(kernel, ntier, ntile, nblk, group),
            out_shape=(vm(temp.shape), vm((1, nblk)), vm((lev, width))),
            in_specs=[pl.BlockSpec(memory_space=pltpu.HBM)] * 7,
            out_specs=(vmem, vmem, vmem),
            scratch_shapes=[
                vm(temp.shape), vm(mats.shape, i32), vm(rates.shape),
                pltpu.SMEM(labels.shape, i32), vm(stat.shape), vm(fac.shape), vm(op.shape),
                dma((7,)),
                vm(block), vm(block, i32), vm((2, levels, C)), vm((2, levels, C), i32), vm((2, levels, C)),
                vm((nwin, 2, 8, C)), vm((group, ntier, 2, 8, C)), vm((2, ntier, 2, 8, C)),
                vm((grows + 1, levels, C)), vm(block), vm(block), vm((levels, (grows + 1) * C)),
                vm(block), vm((levels, C)), vm(block),
                vm((nwin, 8, pad)), vm((ngrp, 8, pad)), vm((nwin, 8, pad)), vm((ngrp, 8, pad)),
                dma, dma, dma, dma,
                dma((group,)), dma((group,)), dma((group,)), dma((group,)), dma, dma((group,)), dma, dma, dma,
                dma((4, 2)), dma((4, 2)),
                dma, dma, dma, dma, dma, dma, dma, dma, pltpu.SemaphoreType.REGULAR,
            ],
            compiler_params=pltpu.CompilerParams(
                collective_id=0, has_side_effects=True, vmem_limit_bytes=48 * 1024 * 1024
            ),
        )(*args)
        anywhere = pl.BlockSpec(memory_space=pltpu.HBM)
        return pl.pallas_call(
            last,
            out_shape=(
                jax.ShapeDtypeStruct(temp.shape, f32),
                jax.ShapeDtypeStruct((1, nblk), f32),
            ),
            in_specs=[vmem] * 3,
            out_specs=(anywhere, anywhere),
            scratch_shapes=[vm(temp.shape), dma((rows + 1,))],
            compiler_params=pltpu.CompilerParams(vmem_limit_bytes=4 * 1024 * 1024),
        )(field, lift, power)

    return jax.shard_map(
        shards,
        mesh=mesh,
        in_specs=(P("tile", "tier", None), P("tile", "tier", None), P(), P("tile", None), P(), P(), P()),
        out_specs=(P("tile", "tier", None), P("tier", None)),
        check_vma=False,
    )
```

```python
import functools

import jax
import jax.numpy as jnp
from jax import lax
from jax.experimental import pallas as pl
from jax.experimental.pallas import tpu as pltpu
from jax.sharding import PartitionSpec as P

C = 128
RATE = 0.12
SOURCE_GAIN = 0.02
MESH = pl.DeviceIdType.MESH


def split(x):
    high = x.astype(jnp.bfloat16)
    return high, (x - high.astype(jnp.float32)).astype(jnp.bfloat16)


def solve(op, x):
    high, low = split(x)
    n = op.shape[0] // 2
    both = jnp.dot(op, high, preferred_element_type=jnp.float32)
    more = jnp.dot(op[:n], low, preferred_element_type=jnp.float32)
    return both[:n] + (both[n:] + more)


def roll(x, shift):
    return pltpu.roll(x, shift % C, x.ndim - 1) if shift % C else x


def kernel(
    ntier, ntile, nblk, group,
    t_hbm, m_hbm, rates_hbm, labels_hbm, stat_hbm, fac_hbm, a_hbm,
    out, pw_out, lift_out,
    t_in, m_in, rates, labels, stat, fac, a_in, s_in,
    col_t, col_m, halo_t, halo_m, halo_1,
    pk_out, pk, halo_p,
    cx, cy, ce, mv, t1, t1c, res,
    p1g, p1z, p2,
    s_t, s_m, s_pk, s_o,
    r_et, r_em, r_at, r_im, r_it, r_rt, r_rm, r_pk, r_o,
    s_h, r_h,
    s_p1g, r_p1g, s_p1z, r_p1z, s_p2, r_p2, entered,
):
    tier = lax.axis_index("tier")
    tile = lax.axis_index("tile")
    rows, lev, width = t_in.shape
    levels = lev * ntier
    nmat = rates.shape[1]
    ngrp = ntile // group
    grows = rows * group
    sub = lax.rem(tile, group)
    base = tile - sub
    place = tile // group
    own = tier * group + sub
    nwin = ntier * group
    active_rows = [t * lev for t in range(ntier)]

    loads = [
        pltpu.make_async_copy(src, dst, s_in.at[i])
        for i, (src, dst) in enumerate(
            ((t_hbm, t_in), (m_hbm, m_in), (labels_hbm, labels), (rates_hbm, rates),
             (stat_hbm, stat), (fac_hbm, fac), (a_hbm, a_in))
        )
    ]
    for load in loads:
        load.start()

    peers = []
    for a in range(ntier):
        for b in range(group):
            t2 = lax.rem(tier + a, ntier)
            s2 = lax.rem(sub + b, group)
            peers.append((a == 0 and b == 0, t2, s2))

    def there(t2, s2):
        return {"tier": t2, "tile": base + s2}

    barrier = pltpu.get_barrier_semaphore()
    for mine, t2, s2 in peers:
        if not mine:
            pl.semaphore_signal(barrier, inc=1, device_id=there(t2, s2), device_id_type=MESH)

    def across(k):
        return {"tile": lax.rem(tile + k * group, ntile)}

    def greet(sem, low, high):
        def one(k, carry):
            pl.semaphore_signal(
                sem, inc=1, device_id={"tile": k * group + sub}, device_id_type=MESH
            )
            return carry

        lax.fori_loop(low, high, one, 0)

    greet(barrier, place + 1, ngrp)

    def cols(w):
        return pl.ds(pl.multiple_of(w * C, C), C)

    def levs(t):
        return pl.ds(pl.multiple_of(t * lev, 8), lev)

    lane = lax.broadcasted_iota(jnp.int32, (1, C), 1)
    blk = lax.broadcasted_iota(jnp.int32, (1, nblk), 1)

    for load in loads:
        load.wait()

    note = lax.broadcasted_iota(jnp.int32, p1g.shape[1:], 1)
    line = jnp.zeros(p1g.shape[1:], jnp.float32)
    active = t_in[0, 0:1, :]
    for r in range(1, rows):
        active = active + t_in[r, 0:1, :]
    for j in range(width // C):
        label = labels[0, j]
        part = jnp.sum(active[:, j * C : (j + 1) * C], axis=1, keepdims=True)
        line = line + jnp.where(note == label, part, 0.0)
        line = line + jnp.where(note == nblk + label, float(rows * C), 0.0)
        line = jnp.where(note == 2 * nblk + j, label.astype(jnp.float32), line)
    p1g[own] = line

    pl.semaphore_wait(barrier, nwin - 1 + place)
    greet(entered, 0, place)

    def group_send(buf, s_sem, r_sem):
        for mine, t2, s2 in peers:
            if not mine:
                pltpu.make_async_remote_copy(
                    src_ref=buf.at[own], dst_ref=buf.at[own], send_sem=s_sem, recv_sem=r_sem,
                    device_id=there(t2, s2), device_id_type=MESH,
                ).start()

    def across_send(buf, s_sem, r_sem):
        def send(k, carry):
            pltpu.make_async_remote_copy(
                src_ref=buf.at[0], dst_ref=buf.at[k], send_sem=s_sem, recv_sem=r_sem,
                device_id=across(k), device_id_type=MESH,
            ).start()
            return carry

        lax.fori_loop(1, ngrp, send, 0)

    def wait_for(ref, sem):
        pltpu.make_async_copy(ref, ref, sem).wait()

    def all_but_one(buf, sem):
        wait_for(buf.at[pl.ds(1, buf.shape[0] - 1)], sem)

    def total(buf):
        return lax.fori_loop(1, ngrp, lambda k, acc: acc + buf[k], buf[0])

    group_send(p1g, s_p1g, r_p1g)

    def spread(src, dst, row, to, count, s_sem, r_sem):
        for mine, t2, s2 in peers:
            src_ref = src.at[pl.ds(row, count), :, cols(t2 * group + s2)]
            dst_ref = dst.at[pl.ds(to, count), levs(tier), :]
            if mine:
                pltpu.make_async_copy(src_ref, dst_ref, r_sem).start()
            else:
                pltpu.make_async_remote_copy(
                    src_ref=src_ref, dst_ref=dst_ref, send_sem=s_sem, recv_sem=r_sem,
                    device_id=there(t2, s2), device_id_type=MESH,
                ).start()

    edge = lax.select(sub == 0, 0, rows - 1)
    beside = lax.select(sub == 0, 1, rows - 2)
    other = lax.select(sub == 0, rows - 2, 1)
    inmost = lax.select(sub == 0, rows - 1, 0)
    spread(t_hbm, col_t, edge, sub * rows + edge, 1, s_t, r_et.at[sub])
    spread(m_hbm, col_m, edge, sub * rows + edge, 1, s_m, r_em.at[sub])

    quad = lane >> 2
    for w in range(nwin):
        low = max(w - 1, 0) * C
        high = min(w + 1, nwin - 1) * C
        first = second = None
        for g in range(lev // 8):
            ls = slice(8 * g, 8 * g + 8)
            for q, src in ((0, t_in), (rows, m_in)):
                for r in range(rows):
                    both = jnp.where(
                        lane >= 64, src[r, ls, low : low + C], src[r, ls, high : high + C]
                    )
                    if q:
                        both = both.astype(jnp.float32)
                    put = roll(both, 32 * g + 4 * (q + r) + 2)
                    first = put if first is None else jnp.where(quad == 8 * g + q + r, put, first)
            whole = None
            for r in range(rows):
                block = t_in[r, ls, w * C : (w + 1) * C]
                whole = block if whole is None else whole + block
                put = roll(block, 32 * g + 4 * r + 2)
                second = put if second is None else jnp.where(quad == 8 * g + r, put, second)
                put = roll(
                    m_in[r, ls, w * C : (w + 1) * C].astype(jnp.float32), 32 * g + 4 * (rows + r) + 2
                )
                second = jnp.where(quad == 8 * g + rows + r, put, second)
            whole = jnp.sum(whole, axis=1, keepdims=True)
            second = jnp.where(lane == 32 * g + 3, whole, second)
        pk_out[w, 0] = first
        pk_out[w, 1] = second

    for mine, t2, s2 in peers:
        src_ref, dst_ref = pk_out.at[t2 * group + s2], pk.at[sub, tier]
        if mine:
            pltpu.make_async_copy(src_ref, dst_ref, r_pk).start()
        else:
            pltpu.make_async_remote_copy(
                src_ref=src_ref, dst_ref=dst_ref, send_sem=s_pk, recv_sem=r_pk,
                device_id=there(t2, s2), device_id_type=MESH,
            ).start()
    spread(m_hbm, col_m, inmost, sub * rows + inmost, 1, s_m, r_im)
    spread(t_hbm, col_t, inmost, sub * rows + inmost, 1, s_t, r_it)
    spread(m_hbm, col_m, 1, sub * rows + 1, rows - 2, s_m, r_rm.at[sub])
    spread(t_hbm, col_t, beside, sub * rows + beside, 1, s_t, r_at.at[sub])
    spread(t_hbm, col_t, other, sub * rows + other, 1, s_t, r_rt.at[sub])

    has_low = place > 0
    has_high = place < ngrp - 1

    @pl.when(jnp.logical_not(has_low))
    def _():
        for ref in (halo_t, halo_m, halo_p, halo_1):
            ref[0] = jnp.zeros(ref.shape[1:], ref.dtype)

    @pl.when(jnp.logical_not(has_high))
    def _():
        for ref in (halo_t, halo_m, halo_p, halo_1):
            ref[1] = jnp.zeros(ref.shape[1:], ref.dtype)

    def halo(low_src, high_src, dst, which):
        down = pltpu.make_async_remote_copy(
            src_ref=low_src, dst_ref=dst.at[1],
            send_sem=s_h.at[which, 0], recv_sem=r_h.at[which, 1],
            device_id={"tile": lax.max(tile - group, sub)}, device_id_type=MESH,
        )
        up = pltpu.make_async_remote_copy(
            src_ref=high_src, dst_ref=dst.at[0],
            send_sem=s_h.at[which, 1], recv_sem=r_h.at[which, 0],
            device_id={"tile": lax.min(tile + group, ntile - group + sub)}, device_id_type=MESH,
        )
        return down, up

    def halo_recv(copies):
        pl.when(has_low)(lambda: copies[1].wait_recv())
        pl.when(has_high)(lambda: copies[0].wait_recv())

    def halo_sent(copies):
        pl.when(has_low)(lambda: copies[0].wait_send())
        pl.when(has_high)(lambda: copies[1].wait_send())

    h_t = halo(col_t.at[0], col_t.at[grows - 1], halo_t, 0)
    h_m = halo(col_m.at[0], col_m.at[grows - 1], halo_m, 1)
    h_p = halo(pk.at[0, :, 0], pk.at[group - 1, :, 0], halo_p, 2)
    h_1 = halo(t1.at[0], t1.at[grows - 1], halo_1, 3)

    all_but_one(p1g, r_p1g)
    p1z[0] = jnp.zeros(p1z.shape[1:], jnp.float32)
    for t in range(ntier):
        acc = p1g[t * group]
        for s in range(1, group):
            acc = acc + p1g[t * group + s]
        p1z[0, t : t + 1, :] = acc
    pl.when(has_high)(lambda: pl.semaphore_wait(entered, ngrp - 1 - place))
    across_send(p1z, s_p1z, r_p1z)

    for s, row in ((0, 0), (group - 1, grows - 1)):
        wait_for(col_t.at[row], r_et.at[s])
        wait_for(col_m.at[row], r_em.at[s])
    pl.when(has_low)(lambda: (h_m[0].start(), h_t[0].start()) and None)
    pl.when(has_high)(lambda: (h_m[1].start(), h_t[1].start()) and None)
    wait_for(pk, r_pk)
    pl.when(has_low)(lambda: h_p[0].start())
    pl.when(has_high)(lambda: h_p[1].start())

    inverse = 1.0 / ((2.0 * RATE) * rates[...])
    table = [
        [jnp.broadcast_to(inverse[a : a + 1, m : m + 1], (1, C)) for m in range(nmat)]
        for a in range(2)
    ]

    def lookup(codes, axes):
        outs = [jnp.broadcast_to(table[a][0], codes.shape) for a in axes]
        for m in range(1, nmat):
            hit = codes == m
            outs = [jnp.where(hit, table[a][m], o) for a, o in zip(axes, outs)]
        return outs

    def unpack(low, high, shift_low, shift_high, split):
        pieces = []
        for t in range(ntier):
            for g in range(lev // 8):
                a = roll(low(t), shift_low - 32 * g)
                if high is not None:
                    a = jnp.where(lane < split, a, roll(high(t), shift_high - 32 * g))
                pieces.append(a)
        return jnp.concatenate(pieces, axis=0)

    def swap(x):
        return jnp.where((lane & 3) == 1, roll(x, -1), roll(x, 1))

    half = 4 * rows
    out_t = unpack(lambda t: pk[0, t, 0], lambda t: pk[1, t, 0], 0, half, half)
    out_m = unpack(lambda t: pk[0, t, 0], lambda t: pk[1, t, 0], -half, 0, half)
    own_t = unpack(lambda t: pk[0, t, 1], lambda t: pk[1, t, 1], 0, half, half)
    own_m = unpack(lambda t: pk[0, t, 1], lambda t: pk[1, t, 1], -half, 0, half)
    ixc, iyc = lookup(out_m, (0, 1))
    (iyo,) = lookup(own_m, (1,))
    pos_low = (lane & 3) == 1

    op_active = [a_in[:, a : a + 1] for a in active_rows]
    op = jnp.concatenate(split(a_in[...]), axis=0)

    there_is = jnp.where(pos_low, jnp.where(own > 0, 1.0, 0.0), jnp.where(own < nwin - 1, 1.0, 0.0))
    c_in = there_is / (iyc + swap(iyo))
    c_far = 1.0 / (iyc + jnp.where(pos_low, roll(iyc, 1), roll(iyc, -1)))
    into_side = c_in * (swap(own_t) - out_t)
    spun = swap(c_in)
    kx = {}

    def conduct(r):
        kx[r], iy = lookup(col_m[r], (0, 1))
        ce[r] = roll(spun, -(4 * r + 2))
        cy[r] = jnp.where(lane == C - 1, ce[r], 1.0 / (iy + roll(iy, -1)))
        for q in (r, r + 1):
            if q - 1 in kx and q in kx:
                cx[q] = 1.0 / (kx[q - 1] + kx[q])

    outer = [0, grows - 1]
    near = [1, grows - 2]
    middle = list(range(2, grows - 2))
    for r in outer:
        conduct(r)
    wait_for(col_m.at[pl.ds(rows - 1, 2)], r_im)
    for r in (rows - 1, rows):
        conduct(r)

    all_but_one(p1z, r_p1z)
    whole = total(p1z)
    count = whole[0:1, nblk : 2 * nblk]
    power = stat[...] * jnp.exp(fac[...] * whole[0:ntier, 0:nblk] / count)

    def label_of(s, w):
        return jnp.sum(jnp.where(note == 2 * nblk + w, p1g[s], 0.0), axis=1, keepdims=True)

    blkf = blk.astype(jnp.float32)

    def gain_of(pw, label):
        return SOURCE_GAIN * jnp.sum(jnp.where(blkf == label, pw, 0.0), axis=1, keepdims=True)

    own_labels = [label_of(s, own) for s in range(group)]
    gains = [gain_of(power, label) for label in own_labels]
    lift = []
    for s in range(group):
        acc = op_active[0] * gains[s][0:1, :]
        for t in range(1, ntier):
            acc = acc + op_active[t] * gains[s][t : t + 1, :]
        lift.append(acc)
    side = jnp.zeros((ntier, C), jnp.float32)
    for s in range(group):
        gl = gain_of(power, label_of(s, own - 1))
        gr = gain_of(power, label_of(s, own + 1))
        side = jnp.where(lane // half == s, jnp.where(pos_low, gl, gr), side)
    lift_c = op_active[0] * side[0:1, :]
    for t in range(1, ntier):
        lift_c = lift_c + op_active[t] * side[t : t + 1, :]

    for s in range(group):
        wait_for(col_m.at[pl.ds(s * rows + 1, rows - 2)], r_rm.at[s])
    for s in range(group):
        for r in range(s * rows + 1, (s + 1) * rows - 1):
            conduct(r)
    first, last = kx[0], kx[grows - 1]

    halo_recv(h_m)
    halo_recv(h_p)
    (ix,) = lookup(halo_m[0], (0,))
    cx[0] = jnp.where(has_low, 1.0 / (ix + first), 0.0)
    (ix,) = lookup(halo_m[1], (0,))
    cx[grows] = jnp.where(has_high, 1.0 / (ix + last), 0.0)

    end = 4 * (rows - 1)
    up_t = unpack(lambda t: halo_p[0, t], None, -end, 0, 0)
    up_m = unpack(lambda t: halo_p[0, t], None, -end - half, 0, 0)
    dn_t = unpack(lambda t: halo_p[1, t], None, 4 * (grows - 1), 0, 0)
    dn_m = unpack(lambda t: halo_p[1, t], None, 4 * (grows - 1) - half, 0, 0)
    (up_ix,) = lookup(up_m, (0,))
    (dn_ix,) = lookup(dn_m, (0,))
    at_top = lane < 4
    at_bottom = lane >= 4 * (grows - 1)
    up_c = 1.0 / (ixc + jnp.where(at_top, up_ix, roll(ixc, 4)))
    up_c = jnp.where(jnp.logical_and(at_top, jnp.logical_not(has_low)), 0.0, up_c)
    dn_c = 1.0 / (ixc + jnp.where(at_bottom, dn_ix, roll(ixc, -4)))
    dn_c = jnp.where(jnp.logical_and(at_bottom, jnp.logical_not(has_high)), 0.0, dn_c)
    part = (
        out_t
        + up_c * (jnp.where(at_top, up_t, roll(out_t, 4)) - out_t)
        + dn_c * (jnp.where(at_bottom, dn_t, roll(out_t, -4)) - out_t)
        + into_side
        + c_far * (jnp.where(pos_low, roll(out_t, 1), roll(out_t, -1)) - out_t)
    )


    def lateral(field, outside, r, above, below):
        here = field[r]
        edge_in = roll(outside, -(4 * r + 2))
        beside = jnp.where(lane == C - 1, edge_in, roll(here, -1))
        flux = cy[r] * (beside - here)
        left = jnp.where(lane == 0, ce[r] * (here - edge_in), roll(flux, 1))
        moved = here + (flux - left)
        return moved + cx[r + 1] * (below - here) - cx[r] * (here - above)

    halo_recv(h_t)
    spun = swap(out_t)
    place_of = {r: i for i, r in enumerate(outer + [grows] + list(range(1, grows - 1)))}

    def at(r, n=1):
        return slice(place_of[r] * C, (place_of[r] + n) * C)

    def first_move(r):
        above = halo_t[0] if r == 0 else col_t[r - 1]
        below = halo_t[1] if r == grows - 1 else col_t[r + 1]
        mv[:, at(r)] = lateral(col_t, spun, r, above, below)

    wait_for(col_t.at[pl.ds(rows - 1, 2)], r_it)
    flows = [
        cx[0] * (halo_t[0] - col_t[0]),
        cx[rows] * (col_t[rows] - col_t[rows - 1]),
        cx[grows] * (halo_t[1] - col_t[grows - 1]),
    ]
    inflow = (flows[0] + flows[1], flows[2] - flows[1])
    side_lane = jnp.logical_or((lane & 3) == 1, (lane & 3) == 2)
    stock = []
    for s in range(group):
        mine = jnp.logical_and(lane // half == s, side_lane)
        stock.append(
            inflow[s]
            - jnp.where(mine, into_side, 0.0)
            + jnp.where(lane == s * half + 3, own_t, 0.0)
        )
    n_act = -(-ntier // 8) * 8
    act = jnp.concatenate(
        [a_in[a : a + 1, :] for a in active_rows]
        + [jnp.zeros((n_act - ntier, levels), jnp.float32)], axis=0
    )
    found = solve(jnp.concatenate(split(act), axis=0), jnp.concatenate(stock, axis=1))
    slot = place * nwin + own
    note2 = lax.broadcasted_iota(jnp.int32, p2.shape[1:], 1)
    line = jnp.zeros(p2.shape[1:], jnp.float32)
    for s in range(group):
        acc = jnp.sum(found[0:ntier, s * C : (s + 1) * C], axis=1, keepdims=True)
        acc = acc + float(rows * C) * jnp.concatenate(
            [lift[s][a : a + 1, :] for a in active_rows], axis=0
        )
        name = own_labels[s].astype(jnp.int32)
        for t in range(ntier):
            line = line + jnp.where(note2 == t * nblk + name, acc[t : t + 1, :], 0.0)
    p2[slot] = line

    def to_all(t2, tile2):
        pltpu.make_async_remote_copy(
            src_ref=p2.at[slot], dst_ref=p2.at[slot], send_sem=s_p2, recv_sem=r_p2,
            device_id={"tier": t2, "tile": tile2}, device_id_type=MESH,
        ).start()

    def to_group(k, carry):
        for _, t2, s2 in peers:
            to_all(t2, lax.rem(base + k * group, ntile) + s2)
        return carry

    lax.fori_loop(1, ngrp, to_group, 0)
    for mine, t2, s2 in peers:
        if not mine:
            to_all(t2, base + s2)

    for s, row in ((0, 1), (group - 1, grows - 2)):
        wait_for(col_t.at[row], r_at.at[s])
    for r in outer:
        first_move(r)
    mv[:, at(grows)] = part
    both = solve(op, mv[:, at(0, 3)])
    for i, r in enumerate(outer):
        t1[r] = both[:, i * C : (i + 1) * C] + lift[r // rows]
    t1c = both[:, 2 * C :] + lift_c
    pl.when(has_low)(lambda: h_1[0].start())
    pl.when(has_high)(lambda: h_1[1].start())

    for s, row in ((0, rows - 2), (group - 1, rows + 1)):
        wait_for(col_t.at[row], r_rt.at[s])
    for r in near + middle:
        first_move(r)
    most = solve(op, mv[:, at(1, grows - 2)])
    for r in range(1, grows - 1):
        t1[r] = most[:, (r - 1) * C : r * C] + lift[r // rows]

    def send_rows(s, first_row, count):
        for t in range(ntier):
            for_me = jnp.logical_and(tier == t, sub == s)
            src_ref = res.at[pl.ds(s * rows + first_row, count), pl.ds(t * lev, lev), :]
            dst_ref = out.at[pl.ds(first_row, count), :, cols(own)]

            @pl.when(for_me)
            def _():
                pltpu.make_async_copy(src_ref, dst_ref, r_o).start()

            @pl.when(jnp.logical_not(for_me))
            def _():
                pltpu.make_async_remote_copy(
                    src_ref=src_ref, dst_ref=dst_ref, send_sem=s_o, recv_sem=r_o,
                    device_id=there(t, s), device_id_type=MESH,
                ).start()

    spun = swap(t1c)

    def finish(rs):
        for r in rs:
            above = halo_1[0] if r == 0 else t1[r - 1]
            below = halo_1[1] if r == grows - 1 else t1[r + 1]
            mv[:, at(r)] = lateral(t1, spun, r, above, below)
        x = solve(op, mv[:, at(rs[0], len(rs))])
        for i, r in enumerate(rs):
            res[r] = x[:, i * C : (i + 1) * C]

    for s in range(group):
        finish(list(range(s * rows + (s == 0), (s + 1) * rows - (s == group - 1))))
        send_rows(s, int(s == 0), rows - 1)

    halo_recv(h_1)
    finish(outer)
    for s, r in ((0, 0), (group - 1, grows - 1)):
        send_rows(s, r - s * rows, 1)

    all_but_one(p2, r_p2)
    whole = jnp.sum(p2[...], axis=0)
    whole = jnp.concatenate([whole[:, t * nblk : (t + 1) * nblk] for t in range(ntier)], axis=0)
    power = stat[...] * jnp.exp(fac[...] * whole[0:ntier, 0:nblk] / count)
    mine = lax.broadcasted_iota(jnp.int32, (ntier, nblk), 0) == tier
    pw_out[...] = jnp.sum(jnp.where(mine, power, 0.0), axis=0, keepdims=True)
    own_op = a_in[levs(tier), :]
    for j in range(width // C):
        g = SOURCE_GAIN * jnp.sum(jnp.where(blk == labels[0, j], power, 0.0), axis=1, keepdims=True)
        acc = own_op[:, active_rows[0] : active_rows[0] + 1] * g[0:1, :]
        for t in range(1, ntier):
            a = active_rows[t]
            acc = acc + own_op[:, a : a + 1] * g[t : t + 1, :]
        lift_out[:, j * C : (j + 1) * C] = jnp.broadcast_to(acc, (lev, C))
    wait_for(out, r_o)

    for copies in (h_t, h_m, h_p, h_1):
        halo_sent(copies)
    sent = pl.ds(0, nwin - 1)
    wait_for(res.at[sent], s_t)
    wait_for(res.at[sent], s_m)
    wait_for(res.at[sent], s_o)
    wait_for(pk_out.at[sent], s_pk)
    all_but_one(p1g, s_p1g)
    all_but_one(p1z, s_p1z)
    all_but_one(p2, s_p2)


def last(field, lift, power, out, power_out, done, sem):
    copies = []
    for r in range(field.shape[0]):
        done[r] = field[r] + lift[...]
        copies.append(pltpu.make_async_copy(done.at[r], out.at[r], sem.at[r]))
        copies[-1].start()
    copies.append(pltpu.make_async_copy(power, power_out, sem.at[field.shape[0]]))
    copies[-1].start()
    for copy in copies:
        copy.wait()


def solution(mesh):
    ntier, ntile = mesh.shape["tier"], mesh.shape["tile"]

    def shards(temp, mats, rates, labels, stat, fac, op):
        rows, lev, width = temp.shape
        nblk = stat.shape[1]
        pad = lambda n: -(-n // C) * C
        group = width // (ntier * C)
        levels, grows, ngrp, nwin = lev * ntier, rows * group, ntile // group, width // C
        f32, i32 = jnp.float32, jnp.int32
        vm = lambda shape, dtype=f32: pltpu.VMEM(shape, dtype)
        dma = pltpu.SemaphoreType.DMA
        vmem = pl.BlockSpec(memory_space=pltpu.VMEM)
        block = (grows, levels, C)
        args = (temp, mats, rates, labels, stat, fac, op)
        args = [pltpu.with_memory_space_constraint(x, pltpu.HBM) for x in args]
        field, power, lift = pl.pallas_call(
            functools.partial(kernel, ntier, ntile, nblk, group),
            out_shape=(vm(temp.shape), vm((1, nblk)), vm((lev, width))),
            in_specs=[pl.BlockSpec(memory_space=pltpu.HBM)] * 7,
            out_specs=(vmem, vmem, vmem),
            scratch_shapes=[
                vm(temp.shape), vm(mats.shape, i32), vm(rates.shape),
                pltpu.SMEM(labels.shape, i32), vm(stat.shape), vm(fac.shape), vm(op.shape),
                dma((7,)),
                vm(block), vm(block, i32), vm((2, levels, C)), vm((2, levels, C), i32), vm((2, levels, C)),
                vm((nwin, 2, 8, C)), vm((group, ntier, 2, 8, C)), vm((2, ntier, 8, C)),
                vm((grows + 1, levels, C)), vm(block), vm(block), vm((levels, (grows + 1) * C)),
                vm(block), vm((levels, C)), vm(block),
                vm((nwin, 1, pad(2 * nblk + nwin))), vm((ngrp, 8, pad(2 * nblk + nwin))),
                vm((ngrp * nwin, 1, pad(ntier * nblk))),
                dma, dma, dma, dma,
                dma((group,)), dma((group,)), dma((group,)), dma, dma, dma((group,)), dma((group,)), dma, dma,
                dma((4, 2)), dma((4, 2)),
                dma, dma, dma, dma, dma, dma, pltpu.SemaphoreType.REGULAR,
            ],
            compiler_params=pltpu.CompilerParams(
                collective_id=0, has_side_effects=True, vmem_limit_bytes=48 * 1024 * 1024
            ),
        )(*args)
        anywhere = pl.BlockSpec(memory_space=pltpu.HBM)
        return pl.pallas_call(
            last,
            out_shape=(
                jax.ShapeDtypeStruct(temp.shape, f32),
                jax.ShapeDtypeStruct((1, nblk), f32),
            ),
            in_specs=[vmem] * 3,
            out_specs=(anywhere, anywhere),
            scratch_shapes=[vm(temp.shape), dma((rows + 1,))],
            compiler_params=pltpu.CompilerParams(vmem_limit_bytes=4 * 1024 * 1024),
        )(field, lift, power)

    return jax.shard_map(
        shards,
        mesh=mesh,
        in_specs=(P("tile", "tier", None), P("tile", "tier", None), P(), P("tile", None), P(), P(), P()),
        out_specs=(P("tile", "tier", None), P("tier", None)),
        check_vma=False,
    )
```

```python
import functools

import jax
import jax.numpy as jnp
from jax import lax
from jax.experimental import pallas as pl
from jax.experimental.pallas import tpu as pltpu
from jax.sharding import PartitionSpec as P

C = 128
RATE = 0.12
SOURCE_GAIN = 0.02
MESH = pl.DeviceIdType.MESH


def split(x):
    high = x.astype(jnp.bfloat16)
    return high, (x - high.astype(jnp.float32)).astype(jnp.bfloat16)


def solve(op, x):
    high, low = split(x)
    n = op.shape[0] // 2
    both = jnp.dot(op, high, preferred_element_type=jnp.float32)
    more = jnp.dot(op[:n], low, preferred_element_type=jnp.float32)
    return both[:n] + (both[n:] + more)


def roll(x, shift):
    return pltpu.roll(x, shift % C, x.ndim - 1) if shift % C else x


def kernel(
    ntier, ntile, nblk, group,
    t_hbm, m_hbm, rates_hbm, labels_hbm, stat_hbm, fac_hbm, a_hbm,
    out, pw_out, lift_out,
    t_in, m_in, rates, labels, stat, fac, a_in, s_in,
    col_t, col_m, halo_t, halo_m, halo_1,
    pk_out, pk, halo_p,
    cx, cy, ce, mv, t1, t1c, res,
    p1g, p1z, p2,
    s_t, s_m, s_pk, s_o,
    r_et, r_em, r_bt, r_bm, r_it, r_im, r_om, r_rt, r_pk, r_o,
    s_h, r_h,
    s_p1g, r_p1g, s_p1z, r_p1z, s_p2, r_p2, entered,
):
    tier = lax.axis_index("tier")
    tile = lax.axis_index("tile")
    rows, lev, width = t_in.shape
    levels = lev * ntier
    nmat = rates.shape[1]
    ngrp = ntile // group
    grows = rows * group
    sub = lax.rem(tile, group)
    base = tile - sub
    place = tile // group
    own = tier * group + sub
    nwin = ntier * group
    active_rows = [t * lev for t in range(ntier)]

    loads = [
        pltpu.make_async_copy(src, dst, s_in.at[i])
        for i, (src, dst) in enumerate(
            ((t_hbm, t_in), (m_hbm, m_in), (labels_hbm, labels), (rates_hbm, rates),
             (stat_hbm, stat), (fac_hbm, fac), (a_hbm, a_in))
        )
    ]
    for load in loads:
        load.start()

    turned = tier + 1 - 2 * lax.rem(tier, 2)
    peers = []
    for b in range(group - 1, -1, -1):
        for a in range(ntier - 2, -1, -2):
            for start in (tier, turned):
                mine = a == 0 and b == 0 and start is tier
                peers.append((mine, lax.rem(start + a, ntier), lax.rem(sub + b, group)))

    def there(t2, s2):
        return {"tier": t2, "tile": base + s2}

    barrier = pltpu.get_barrier_semaphore()
    for mine, t2, s2 in peers:
        if not mine:
            pl.semaphore_signal(barrier, inc=1, device_id=there(t2, s2), device_id_type=MESH)

    def across(k):
        return {"tile": lax.rem(tile + k * group, ntile)}

    def greet(sem, low, high):
        def one(k, carry):
            pl.semaphore_signal(
                sem, inc=1, device_id={"tile": k * group + sub}, device_id_type=MESH
            )
            return carry

        lax.fori_loop(low, high, one, 0)

    greet(barrier, place + 1, ngrp)

    def cols(w):
        return pl.ds(pl.multiple_of(w * C, C), C)

    def levs(t):
        return pl.ds(pl.multiple_of(t * lev, 8), lev)

    lane = lax.broadcasted_iota(jnp.int32, (1, C), 1)
    blk = lax.broadcasted_iota(jnp.int32, (1, nblk), 1)

    for load in loads:
        load.wait()

    note = lax.broadcasted_iota(jnp.int32, p1g.shape[1:], 1)
    line = jnp.zeros(p1g.shape[1:], jnp.float32)
    active = t_in[0, 0:1, :]
    for r in range(1, rows):
        active = active + t_in[r, 0:1, :]
    for j in range(width // C):
        label = labels[0, j]
        part = jnp.sum(active[:, j * C : (j + 1) * C], axis=1, keepdims=True)
        line = line + jnp.where(note == label, part, 0.0)
        line = line + jnp.where(note == nblk + label, float(rows * C), 0.0)
        line = jnp.where(note == 2 * nblk + j, label.astype(jnp.float32), line)
    p1g[own] = line

    pl.semaphore_wait(barrier, nwin - 1 + place)
    greet(entered, 0, place)

    def group_send(buf, s_sem, r_sem):
        for mine, t2, s2 in peers:
            if not mine:
                pltpu.make_async_remote_copy(
                    src_ref=buf.at[own], dst_ref=buf.at[own], send_sem=s_sem, recv_sem=r_sem,
                    device_id=there(t2, s2), device_id_type=MESH,
                ).start()

    def across_send(buf, s_sem, r_sem):
        def send(k, carry):
            pltpu.make_async_remote_copy(
                src_ref=buf.at[0], dst_ref=buf.at[k], send_sem=s_sem, recv_sem=r_sem,
                device_id=across(k), device_id_type=MESH,
            ).start()
            return carry

        lax.fori_loop(1, ngrp, send, 0)

    def wait_for(ref, sem):
        pltpu.make_async_copy(ref, ref, sem).wait()

    def all_but_one(buf, sem):
        wait_for(buf.at[pl.ds(1, buf.shape[0] - 1)], sem)

    def total(buf):
        return lax.fori_loop(1, ngrp, lambda k, acc: acc + buf[k], buf[0])

    group_send(p1g, s_p1g, r_p1g)

    def spread(src, dst, row, to, count, s_sem, r_sem):
        for mine, t2, s2 in peers:
            src_ref = src.at[pl.ds(row, count), :, cols(t2 * group + s2)]
            dst_ref = dst.at[pl.ds(to, count), levs(tier), :]
            if mine:
                pltpu.make_async_copy(src_ref, dst_ref, r_sem).start()
            else:
                pltpu.make_async_remote_copy(
                    src_ref=src_ref, dst_ref=dst_ref, send_sem=s_sem, recv_sem=r_sem,
                    device_id=there(t2, s2), device_id_type=MESH,
                ).start()

    edge = lax.select(sub == 0, 0, rows - 1)
    beside = lax.select(sub == 0, 1, rows - 2)
    other = lax.select(sub == 0, rows - 2, 1)
    inmost = lax.select(sub == 0, rows - 1, 0)
    spread(t_hbm, col_t, edge, sub * rows + edge, 1, s_t, r_et.at[sub])
    spread(m_hbm, col_m, edge, sub * rows + edge, 1, s_m, r_em.at[sub])

    quad = lane >> 2
    for w in range(nwin):
        low = max(w - 1, 0) * C
        high = min(w + 1, nwin - 1) * C
        first = second = None
        for g in range(lev // 8):
            ls = slice(8 * g, 8 * g + 8)
            for q, src in ((0, t_in), (rows, m_in)):
                for r in range(rows):
                    both = jnp.where(
                        lane >= 64, src[r, ls, low : low + C], src[r, ls, high : high + C]
                    )
                    if q:
                        both = both.astype(jnp.float32)
                    put = roll(both, 32 * g + 4 * (q + r) + 2)
                    first = put if first is None else jnp.where(quad == 8 * g + q + r, put, first)
            whole = None
            for r in range(rows):
                block = t_in[r, ls, w * C : (w + 1) * C]
                whole = block if whole is None else whole + block
                put = roll(block, 32 * g + 4 * r + 2)
                second = put if second is None else jnp.where(quad == 8 * g + r, put, second)
                put = roll(
                    m_in[r, ls, w * C : (w + 1) * C].astype(jnp.float32), 32 * g + 4 * (rows + r) + 2
                )
                second = jnp.where(quad == 8 * g + rows + r, put, second)
            whole = jnp.sum(whole, axis=1, keepdims=True)
            second = jnp.where(lane == 32 * g + 3, whole, second)
        pk_out[w, 0] = first
        pk_out[w, 1] = second

    for mine, t2, s2 in peers:
        src_ref, dst_ref = pk_out.at[t2 * group + s2], pk.at[sub, tier]
        if mine:
            pltpu.make_async_copy(src_ref, dst_ref, r_pk).start()
        else:
            pltpu.make_async_remote_copy(
                src_ref=src_ref, dst_ref=dst_ref, send_sem=s_pk, recv_sem=r_pk,
                device_id=there(t2, s2), device_id_type=MESH,
            ).start()
    spread(m_hbm, col_m, beside, sub * rows + beside, 1, s_m, r_bm.at[sub])
    spread(t_hbm, col_t, beside, sub * rows + beside, 1, s_t, r_bt.at[sub])
    spread(m_hbm, col_m, inmost, sub * rows + inmost, 1, s_m, r_im)
    spread(t_hbm, col_t, inmost, sub * rows + inmost, 1, s_t, r_it)
    spread(m_hbm, col_m, other, sub * rows + other, 1, s_m, r_om.at[sub])
    spread(t_hbm, col_t, other, sub * rows + other, 1, s_t, r_rt.at[sub])

    has_low = place > 0
    has_high = place < ngrp - 1

    @pl.when(jnp.logical_not(has_low))
    def _():
        for ref in (halo_t, halo_m, halo_p, halo_1):
            ref[0] = jnp.zeros(ref.shape[1:], ref.dtype)

    @pl.when(jnp.logical_not(has_high))
    def _():
        for ref in (halo_t, halo_m, halo_p, halo_1):
            ref[1] = jnp.zeros(ref.shape[1:], ref.dtype)

    def halo(low_src, high_src, dst, which):
        down = pltpu.make_async_remote_copy(
            src_ref=low_src, dst_ref=dst.at[1],
            send_sem=s_h.at[which, 0], recv_sem=r_h.at[which, 1],
            device_id={"tile": lax.max(tile - group, sub)}, device_id_type=MESH,
        )
        up = pltpu.make_async_remote_copy(
            src_ref=high_src, dst_ref=dst.at[0],
            send_sem=s_h.at[which, 1], recv_sem=r_h.at[which, 0],
            device_id={"tile": lax.min(tile + group, ntile - group + sub)}, device_id_type=MESH,
        )
        return down, up

    def halo_recv(copies):
        pl.when(has_low)(lambda: copies[1].wait_recv())
        pl.when(has_high)(lambda: copies[0].wait_recv())

    def halo_sent(copies):
        pl.when(has_low)(lambda: copies[0].wait_send())
        pl.when(has_high)(lambda: copies[1].wait_send())

    h_t = halo(col_t.at[0], col_t.at[grows - 1], halo_t, 0)
    h_m = halo(col_m.at[0], col_m.at[grows - 1], halo_m, 1)
    h_p = halo(pk.at[0, :, 0], pk.at[group - 1, :, 0], halo_p, 2)
    h_1 = halo(t1.at[0], t1.at[grows - 1], halo_1, 3)

    all_but_one(p1g, r_p1g)
    p1z[0] = jnp.zeros(p1z.shape[1:], jnp.float32)
    for t in range(ntier):
        acc = p1g[t * group]
        for s in range(1, group):
            acc = acc + p1g[t * group + s]
        p1z[0, t : t + 1, :] = acc
    pl.when(has_high)(lambda: pl.semaphore_wait(entered, ngrp - 1 - place))
    across_send(p1z, s_p1z, r_p1z)

    for s, row in ((0, 0), (group - 1, grows - 1)):
        wait_for(col_t.at[row], r_et.at[s])
        wait_for(col_m.at[row], r_em.at[s])
    pl.when(has_low)(lambda: (h_m[0].start(), h_t[0].start()) and None)
    pl.when(has_high)(lambda: (h_m[1].start(), h_t[1].start()) and None)
    wait_for(pk, r_pk)
    pl.when(has_low)(lambda: h_p[0].start())
    pl.when(has_high)(lambda: h_p[1].start())

    inverse = 1.0 / ((2.0 * RATE) * rates[...])
    table = [
        [jnp.broadcast_to(inverse[a : a + 1, m : m + 1], (1, C)) for m in range(nmat)]
        for a in range(2)
    ]

    def lookup(codes, axes):
        outs = [jnp.broadcast_to(table[a][0], codes.shape) for a in axes]
        for m in range(1, nmat):
            hit = codes == m
            outs = [jnp.where(hit, table[a][m], o) for a, o in zip(axes, outs)]
        return outs

    def unpack(low, high, shift_low, shift_high, split):
        pieces = []
        for t in range(ntier):
            for g in range(lev // 8):
                a = roll(low(t), shift_low - 32 * g)
                if high is not None:
                    a = jnp.where(lane < split, a, roll(high(t), shift_high - 32 * g))
                pieces.append(a)
        return jnp.concatenate(pieces, axis=0)

    def swap(x):
        return jnp.where((lane & 3) == 1, roll(x, -1), roll(x, 1))

    half = 4 * rows
    out_t = unpack(lambda t: pk[0, t, 0], lambda t: pk[1, t, 0], 0, half, half)
    out_m = unpack(lambda t: pk[0, t, 0], lambda t: pk[1, t, 0], -half, 0, half)
    own_t = unpack(lambda t: pk[0, t, 1], lambda t: pk[1, t, 1], 0, half, half)
    own_m = unpack(lambda t: pk[0, t, 1], lambda t: pk[1, t, 1], -half, 0, half)
    ixc, iyc = lookup(out_m, (0, 1))
    (iyo,) = lookup(own_m, (1,))
    pos_low = (lane & 3) == 1

    op_active = [a_in[:, a : a + 1] for a in active_rows]
    op = jnp.concatenate(split(a_in[...]), axis=0)

    there_is = jnp.where(pos_low, jnp.where(own > 0, 1.0, 0.0), jnp.where(own < nwin - 1, 1.0, 0.0))
    c_in = there_is / (iyc + swap(iyo))
    c_far = 1.0 / (iyc + jnp.where(pos_low, roll(iyc, 1), roll(iyc, -1)))
    into_side = c_in * (swap(own_t) - out_t)
    spun_c = swap(c_in)
    kx = {}

    def conduct(r):
        kx[r], iy = lookup(col_m[r], (0, 1))
        ce[r] = roll(spun_c, -(4 * r + 2))
        cy[r] = jnp.where(lane == C - 1, ce[r], 1.0 / (iy + roll(iy, -1)))
        for q in (r, r + 1):
            if q - 1 in kx and q in kx:
                cx[q] = 1.0 / (kx[q - 1] + kx[q])

    outer = [0, grows - 1]
    near = [1, grows - 2]
    middle = list(range(2, grows - 2))
    for r in outer:
        conduct(r)
    for s, r in ((0, 1), (group - 1, grows - 2)):
        wait_for(col_m.at[r], r_bm.at[s])
        conduct(r)
    wait_for(col_m.at[pl.ds(rows - 1, 2)], r_im)
    for r in (rows - 1, rows):
        conduct(r)

    all_but_one(p1z, r_p1z)
    whole = total(p1z)
    count = whole[0:1, nblk : 2 * nblk]
    power = stat[...] * jnp.exp(fac[...] * whole[0:ntier, 0:nblk] / count)

    def label_of(s, w):
        return jnp.sum(jnp.where(note == 2 * nblk + w, p1g[s], 0.0), axis=1, keepdims=True)

    blkf = blk.astype(jnp.float32)

    def gain_of(pw, label):
        return SOURCE_GAIN * jnp.sum(jnp.where(blkf == label, pw, 0.0), axis=1, keepdims=True)

    own_labels = [label_of(s, own) for s in range(group)]
    gains = [gain_of(power, label) for label in own_labels]
    lift = []
    for s in range(group):
        acc = op_active[0] * gains[s][0:1, :]
        for t in range(1, ntier):
            acc = acc + op_active[t] * gains[s][t : t + 1, :]
        lift.append(acc)
    side = jnp.zeros((ntier, C), jnp.float32)
    for s in range(group):
        gl = gain_of(power, label_of(s, own - 1))
        gr = gain_of(power, label_of(s, own + 1))
        side = jnp.where(lane // half == s, jnp.where(pos_low, gl, gr), side)
    lift_c = op_active[0] * side[0:1, :]
    for t in range(1, ntier):
        lift_c = lift_c + op_active[t] * side[t : t + 1, :]

    first, last = kx[0], kx[grows - 1]

    halo_recv(h_m)
    halo_recv(h_p)
    (ix,) = lookup(halo_m[0], (0,))
    cx[0] = jnp.where(has_low, 1.0 / (ix + first), 0.0)
    (ix,) = lookup(halo_m[1], (0,))
    cx[grows] = jnp.where(has_high, 1.0 / (ix + last), 0.0)

    end = 4 * (rows - 1)
    up_t = unpack(lambda t: halo_p[0, t], None, -end, 0, 0)
    up_m = unpack(lambda t: halo_p[0, t], None, -end - half, 0, 0)
    dn_t = unpack(lambda t: halo_p[1, t], None, 4 * (grows - 1), 0, 0)
    dn_m = unpack(lambda t: halo_p[1, t], None, 4 * (grows - 1) - half, 0, 0)
    (up_ix,) = lookup(up_m, (0,))
    (dn_ix,) = lookup(dn_m, (0,))
    at_top = lane < 4
    at_bottom = lane >= 4 * (grows - 1)
    up_c = 1.0 / (ixc + jnp.where(at_top, up_ix, roll(ixc, 4)))
    up_c = jnp.where(jnp.logical_and(at_top, jnp.logical_not(has_low)), 0.0, up_c)
    dn_c = 1.0 / (ixc + jnp.where(at_bottom, dn_ix, roll(ixc, -4)))
    dn_c = jnp.where(jnp.logical_and(at_bottom, jnp.logical_not(has_high)), 0.0, dn_c)
    part = (
        out_t
        + up_c * (jnp.where(at_top, up_t, roll(out_t, 4)) - out_t)
        + dn_c * (jnp.where(at_bottom, dn_t, roll(out_t, -4)) - out_t)
        + into_side
        + c_far * (jnp.where(pos_low, roll(out_t, 1), roll(out_t, -1)) - out_t)
    )


    def lateral(field, outside, r, above, below):
        here = field[r]
        edge_in = roll(outside, -(4 * r + 2))
        beside = jnp.where(lane == C - 1, edge_in, roll(here, -1))
        flux = cy[r] * (beside - here)
        left = jnp.where(lane == 0, ce[r] * (here - edge_in), roll(flux, 1))
        moved = here + (flux - left)
        return moved + cx[r + 1] * (below - here) - cx[r] * (here - above)

    halo_recv(h_t)
    spun = swap(out_t)
    place_of = {r: i for i, r in enumerate(outer + [grows] + near + middle)}

    def at(r, n=1):
        return slice(place_of[r] * C, (place_of[r] + n) * C)

    def first_move(r):
        above = halo_t[0] if r == 0 else col_t[r - 1]
        below = halo_t[1] if r == grows - 1 else col_t[r + 1]
        mv[:, at(r)] = lateral(col_t, spun, r, above, below)

    for s, r in ((0, 1), (group - 1, grows - 2)):
        wait_for(col_t.at[r], r_bt.at[s])
    for r in outer:
        first_move(r)
    mv[:, at(grows)] = part
    both = solve(op, mv[:, at(0, 3)])
    for i, r in enumerate(outer):
        t1[r] = both[:, i * C : (i + 1) * C] + lift[r // rows]
    t1c = both[:, 2 * C :] + lift_c
    pl.when(has_low)(lambda: h_1[0].start())
    pl.when(has_high)(lambda: h_1[1].start())

    wait_for(col_t.at[pl.ds(rows - 1, 2)], r_it)
    flows = [
        cx[0] * (halo_t[0] - col_t[0]),
        cx[rows] * (col_t[rows] - col_t[rows - 1]),
        cx[grows] * (halo_t[1] - col_t[grows - 1]),
    ]
    inflow = (flows[0] + flows[1], flows[2] - flows[1])
    side_lane = jnp.logical_or((lane & 3) == 1, (lane & 3) == 2)
    stock = []
    for s in range(group):
        mine = jnp.logical_and(lane // half == s, side_lane)
        stock.append(
            inflow[s]
            - jnp.where(mine, into_side, 0.0)
            + jnp.where(lane == s * half + 3, own_t, 0.0)
        )
    n_act = -(-ntier // 8) * 8
    act = jnp.concatenate(
        [a_in[a : a + 1, :] for a in active_rows]
        + [jnp.zeros((n_act - ntier, levels), jnp.float32)], axis=0
    )
    found = solve(jnp.concatenate(split(act), axis=0), jnp.concatenate(stock, axis=1))
    slot = place * nwin + own
    note2 = lax.broadcasted_iota(jnp.int32, p2.shape[1:], 1)
    line = jnp.zeros(p2.shape[1:], jnp.float32)
    for s in range(group):
        acc = jnp.sum(found[0:ntier, s * C : (s + 1) * C], axis=1, keepdims=True)
        acc = acc + float(rows * C) * jnp.concatenate(
            [lift[s][a : a + 1, :] for a in active_rows], axis=0
        )
        name = own_labels[s].astype(jnp.int32)
        for t in range(ntier):
            line = line + jnp.where(note2 == t * nblk + name, acc[t : t + 1, :], 0.0)
    p2[slot] = line

    def to_all(t2, tile2):
        pltpu.make_async_remote_copy(
            src_ref=p2.at[slot], dst_ref=p2.at[slot], send_sem=s_p2, recv_sem=r_p2,
            device_id={"tier": t2, "tile": tile2}, device_id_type=MESH,
        ).start()

    def to_group(k, carry):
        for _, t2, s2 in peers:
            to_all(t2, lax.rem(base + k * group, ntile) + s2)
        return carry

    lax.fori_loop(1, ngrp, to_group, 0)
    for mine, t2, s2 in peers:
        if not mine:
            to_all(t2, base + s2)

    for s, r in ((0, rows - 2), (group - 1, rows + 1)):
        wait_for(col_m.at[r], r_om.at[s])
        conduct(r)

    for s, row in ((0, rows - 2), (group - 1, rows + 1)):
        wait_for(col_t.at[row], r_rt.at[s])
    for r in near + middle:
        first_move(r)
    most = solve(op, mv[:, at(1, grows - 2)])
    for i, r in enumerate(near + middle):
        t1[r] = most[:, i * C : (i + 1) * C] + lift[r // rows]

    own_tile, next_tile = peers[-ntier:], peers[:-ntier]

    def send_rows(first_low, first_high, count):
        to_own = lax.select(sub == 0, first_low, first_high)
        to_next = lax.select(sub == 0, first_high, first_low)
        for whom, row in ((next_tile, to_next), (own_tile, to_own)):
            for mine, t2, s2 in whom:
                src_ref = res.at[pl.ds(row, count), levs(t2), :]
                dst_ref = out.at[pl.ds(row - s2 * rows, count), :, cols(own)]
                if mine:
                    pltpu.make_async_copy(src_ref, dst_ref, r_o).start()
                else:
                    pltpu.make_async_remote_copy(
                        src_ref=src_ref, dst_ref=dst_ref, send_sem=s_o, recv_sem=r_o,
                        device_id=there(t2, s2), device_id_type=MESH,
                    ).start()

    spun = swap(t1c)

    def finish(rs):
        for r in rs:
            above = halo_1[0] if r == 0 else t1[r - 1]
            below = halo_1[1] if r == grows - 1 else t1[r + 1]
            mv[:, at(r)] = lateral(t1, spun, r, above, below)
        x = solve(op, mv[:, at(rs[0], len(rs))])
        for i, r in enumerate(rs):
            res[r] = x[:, i * C : (i + 1) * C]

    finish(middle)
    send_rows(2, rows, rows - 2)
    finish(near)
    halo_recv(h_1)
    finish(outer)
    send_rows(0, grows - 2, 2)

    all_but_one(p2, r_p2)
    whole = jnp.sum(p2[...], axis=0)
    whole = jnp.concatenate([whole[:, t * nblk : (t + 1) * nblk] for t in range(ntier)], axis=0)
    power = stat[...] * jnp.exp(fac[...] * whole[0:ntier, 0:nblk] / count)
    mine = lax.broadcasted_iota(jnp.int32, (ntier, nblk), 0) == tier
    pw_out[...] = jnp.sum(jnp.where(mine, power, 0.0), axis=0, keepdims=True)
    own_op = a_in[levs(tier), :]
    for j in range(width // C):
        g = SOURCE_GAIN * jnp.sum(jnp.where(blk == labels[0, j], power, 0.0), axis=1, keepdims=True)
        acc = own_op[:, active_rows[0] : active_rows[0] + 1] * g[0:1, :]
        for t in range(1, ntier):
            a = active_rows[t]
            acc = acc + own_op[:, a : a + 1] * g[t : t + 1, :]
        lift_out[:, j * C : (j + 1) * C] = jnp.broadcast_to(acc, (lev, C))
    wait_for(out, r_o)

    for copies in (h_t, h_m, h_p, h_1):
        halo_sent(copies)
    sent = pl.ds(0, nwin - 1)
    wait_for(res.at[sent], s_t)
    wait_for(res.at[sent], s_m)
    wait_for(res.at[sent], s_o)
    wait_for(pk_out.at[sent], s_pk)
    all_but_one(p1g, s_p1g)
    all_but_one(p1z, s_p1z)
    all_but_one(p2, s_p2)


def last(field, lift, power, out, power_out, done, sem):
    copies = []
    for r in range(field.shape[0]):
        done[r] = field[r] + lift[...]
        copies.append(pltpu.make_async_copy(done.at[r], out.at[r], sem.at[r]))
        copies[-1].start()
    copies.append(pltpu.make_async_copy(power, power_out, sem.at[field.shape[0]]))
    copies[-1].start()
    for copy in copies:
        copy.wait()


def solution(mesh):
    ntier, ntile = mesh.shape["tier"], mesh.shape["tile"]

    def shards(temp, mats, rates, labels, stat, fac, op):
        rows, lev, width = temp.shape
        nblk = stat.shape[1]
        pad = lambda n: -(-n // C) * C
        group = width // (ntier * C)
        levels, grows, ngrp, nwin = lev * ntier, rows * group, ntile // group, width // C
        f32, i32 = jnp.float32, jnp.int32
        vm = lambda shape, dtype=f32: pltpu.VMEM(shape, dtype)
        dma = pltpu.SemaphoreType.DMA
        vmem = pl.BlockSpec(memory_space=pltpu.VMEM)
        block = (grows, levels, C)
        args = (temp, mats, rates, labels, stat, fac, op)
        args = [pltpu.with_memory_space_constraint(x, pltpu.HBM) for x in args]
        field, power, lift = pl.pallas_call(
            functools.partial(kernel, ntier, ntile, nblk, group),
            out_shape=(vm(temp.shape), vm((1, nblk)), vm((lev, width))),
            in_specs=[pl.BlockSpec(memory_space=pltpu.HBM)] * 7,
            out_specs=(pl.BlockSpec(memory_space=pl.ANY), vmem, vmem),
            scratch_shapes=[
                vm(temp.shape), vm(mats.shape, i32), vm(rates.shape),
                pltpu.SMEM(labels.shape, i32), vm(stat.shape), vm(fac.shape), vm(op.shape),
                dma((7,)),
                vm(block), vm(block, i32), vm((2, levels, C)), vm((2, levels, C), i32), vm((2, levels, C)),
                vm((nwin, 2, 8, C)), vm((group, ntier, 2, 8, C)), vm((2, ntier, 8, C)),
                vm((grows + 1, levels, C)), vm(block), vm(block), vm((levels, (grows + 1) * C)),
                vm(block), vm((levels, C)), vm(block),
                vm((nwin, 1, pad(2 * nblk + nwin))), vm((ngrp, 8, pad(2 * nblk + nwin))),
                vm((ngrp * nwin, 1, pad(ntier * nblk))),
                dma, dma, dma, dma,
                dma((group,)), dma((group,)), dma((group,)), dma((group,)), dma, dma, dma((group,)),
                dma((group,)), dma, dma,
                dma((4, 2)), dma((4, 2)),
                dma, dma, dma, dma, dma, dma, pltpu.SemaphoreType.REGULAR,
            ],
            compiler_params=pltpu.CompilerParams(
                collective_id=0, has_side_effects=True, vmem_limit_bytes=48 * 1024 * 1024
            ),
        )(*args)
        anywhere = pl.BlockSpec(memory_space=pltpu.HBM)
        return pl.pallas_call(
            last,
            out_shape=(
                jax.ShapeDtypeStruct(temp.shape, f32),
                jax.ShapeDtypeStruct((1, nblk), f32),
            ),
            in_specs=[vmem] * 3,
            out_specs=(anywhere, anywhere),
            scratch_shapes=[vm(temp.shape), dma((rows + 1,))],
            compiler_params=pltpu.CompilerParams(vmem_limit_bytes=4 * 1024 * 1024),
        )(field, lift, power)

    return jax.shard_map(
        shards,
        mesh=mesh,
        in_specs=(P("tile", "tier", None), P("tile", "tier", None), P(), P("tile", None), P(), P(), P()),
        out_specs=(P("tile", "tier", None), P("tier", None)),
        check_vma=False,
    )
```

```python
import functools

import jax
import jax.numpy as jnp
from jax import lax
from jax.experimental import pallas as pl
from jax.experimental.pallas import tpu as pltpu
from jax.sharding import PartitionSpec as P

C = 128
RATE = 0.12
SOURCE_GAIN = 0.02
MESH = pl.DeviceIdType.MESH


def split(x):
    high = x.astype(jnp.bfloat16)
    return high, (x - high.astype(jnp.float32)).astype(jnp.bfloat16)


def solve(op, x):
    high, low = split(x)
    n = op.shape[0] // 2
    both = jnp.dot(op, high, preferred_element_type=jnp.float32)
    more = jnp.dot(op[:n], low, preferred_element_type=jnp.float32)
    return both[:n] + (both[n:] + more)


def roll(x, shift):
    return pltpu.roll(x, shift % C, x.ndim - 1) if shift % C else x


def kernel(
    ntier, ntile, nblk, group,
    t_hbm, m_hbm, rates_hbm, labels_hbm, stat_hbm, fac_hbm, a_hbm,
    out, pw_out, lift_out,
    t_in, m_in, rates, labels, stat, fac, a_in, s_in,
    col_t, col_m, halo_t, halo_m, halo_1,
    pk_out, pk, halo_p,
    cx, cy, ce, mv, t1, t1c, res,
    p1g, p1z, p2,
    s_t, s_m, s_pk, s_o,
    r_et, r_em, r_bt, r_bm, r_it, r_im, r_om, r_rt, r_pk, r_o,
    s_h, r_h,
    s_p1g, r_p1g, s_p1z, r_p1z, s_p2, r_p2, entered,
):
    tier = lax.axis_index("tier")
    tile = lax.axis_index("tile")
    rows, lev, width = t_in.shape
    levels = lev * ntier
    nmat = rates.shape[1]
    ngrp = ntile // group
    grows = rows * group
    sub = lax.rem(tile, group)
    base = tile - sub
    place = tile // group
    own = tier * group + sub
    nwin = ntier * group
    active_rows = [t * lev for t in range(ntier)]

    loads = [
        pltpu.make_async_copy(src, dst, s_in.at[i])
        for i, (src, dst) in enumerate(
            ((t_hbm, t_in), (m_hbm, m_in), (labels_hbm, labels), (rates_hbm, rates),
             (stat_hbm, stat), (fac_hbm, fac), (a_hbm, a_in))
        )
    ]
    for load in loads:
        load.start()

    turned = tier + 1 - 2 * lax.rem(tier, 2)
    peers = []
    for b in range(group - 1, -1, -1):
        for a in range(ntier - 2, -1, -2):
            for start in (tier, turned):
                mine = a == 0 and b == 0 and start is tier
                peers.append((mine, lax.rem(start + a, ntier), lax.rem(sub + b, group)))

    def there(t2, s2):
        return {"tier": t2, "tile": base + s2}

    barrier = pltpu.get_barrier_semaphore()
    for mine, t2, s2 in peers:
        if not mine:
            pl.semaphore_signal(barrier, inc=1, device_id=there(t2, s2), device_id_type=MESH)

    def across(k):
        return {"tile": lax.rem(tile + k * group, ntile)}

    def greet(sem, low, high):
        def one(k, carry):
            pl.semaphore_signal(
                sem, inc=1, device_id={"tile": k * group + sub}, device_id_type=MESH
            )
            return carry

        lax.fori_loop(low, high, one, 0)

    greet(barrier, place + 1, ngrp)

    def cols(w):
        return pl.ds(pl.multiple_of(w * C, C), C)

    def levs(t):
        return pl.ds(pl.multiple_of(t * lev, 8), lev)

    lane = lax.broadcasted_iota(jnp.int32, (1, C), 1)
    blk = lax.broadcasted_iota(jnp.int32, (1, nblk), 1)

    for load in loads:
        load.wait()

    note = lax.broadcasted_iota(jnp.int32, p1g.shape[1:], 1)
    line = jnp.zeros(p1g.shape[1:], jnp.float32)
    active = t_in[0, 0:1, :]
    for r in range(1, rows):
        active = active + t_in[r, 0:1, :]
    for j in range(width // C):
        label = labels[0, j]
        part = jnp.sum(active[:, j * C : (j + 1) * C], axis=1, keepdims=True)
        line = line + jnp.where(note == label, part, 0.0)
        line = line + jnp.where(note == nblk + label, float(rows * C), 0.0)
        line = jnp.where(note == 2 * nblk + j, label.astype(jnp.float32), line)
    p1g[own] = line

    pl.semaphore_wait(barrier, nwin - 1 + place)
    greet(entered, 0, place)

    def group_send(buf, s_sem, r_sem):
        for mine, t2, s2 in peers:
            if not mine:
                pltpu.make_async_remote_copy(
                    src_ref=buf.at[own], dst_ref=buf.at[own], send_sem=s_sem, recv_sem=r_sem,
                    device_id=there(t2, s2), device_id_type=MESH,
                ).start()

    def across_send(buf, s_sem, r_sem):
        def send(k, carry):
            pltpu.make_async_remote_copy(
                src_ref=buf.at[0], dst_ref=buf.at[k], send_sem=s_sem, recv_sem=r_sem,
                device_id=across(k), device_id_type=MESH,
            ).start()
            return carry

        lax.fori_loop(1, ngrp, send, 0)

    def wait_for(ref, sem):
        pltpu.make_async_copy(ref, ref, sem).wait()

    def all_but_one(buf, sem):
        wait_for(buf.at[pl.ds(1, buf.shape[0] - 1)], sem)

    def total(buf):
        return lax.fori_loop(1, ngrp, lambda k, acc: acc + buf[k], buf[0])

    group_send(p1g, s_p1g, r_p1g)

    def spread(src, dst, row, to, count, s_sem, r_sem):
        for mine, t2, s2 in peers:
            src_ref = src.at[pl.ds(row, count), :, cols(t2 * group + s2)]
            dst_ref = dst.at[pl.ds(to, count), levs(tier), :]
            if mine:
                pltpu.make_async_copy(src_ref, dst_ref, r_sem).start()
            else:
                pltpu.make_async_remote_copy(
                    src_ref=src_ref, dst_ref=dst_ref, send_sem=s_sem, recv_sem=r_sem,
                    device_id=there(t2, s2), device_id_type=MESH,
                ).start()

    edge = lax.select(sub == 0, 0, rows - 1)
    beside = lax.select(sub == 0, 1, rows - 2)
    other = lax.select(sub == 0, rows - 2, 1)
    inmost = lax.select(sub == 0, rows - 1, 0)
    spread(t_hbm, col_t, edge, sub * rows + edge, 1, s_t, r_et.at[sub])
    spread(m_hbm, col_m, edge, sub * rows + edge, 1, s_m, r_em.at[sub])

    quad = lane >> 2
    for w in range(nwin):
        low = max(w - 1, 0) * C
        high = min(w + 1, nwin - 1) * C
        first = second = None
        for g in range(lev // 8):
            ls = slice(8 * g, 8 * g + 8)
            for q, src in ((0, t_in), (rows, m_in)):
                for r in range(rows):
                    both = jnp.where(
                        lane >= 64, src[r, ls, low : low + C], src[r, ls, high : high + C]
                    )
                    if q:
                        both = both.astype(jnp.float32)
                    put = roll(both, 32 * g + 4 * (q + r) + 2)
                    first = put if first is None else jnp.where(quad == 8 * g + q + r, put, first)
            whole = None
            for r in range(rows):
                block = t_in[r, ls, w * C : (w + 1) * C]
                whole = block if whole is None else whole + block
                put = roll(block, 32 * g + 4 * r + 2)
                second = put if second is None else jnp.where(quad == 8 * g + r, put, second)
                put = roll(
                    m_in[r, ls, w * C : (w + 1) * C].astype(jnp.float32), 32 * g + 4 * (rows + r) + 2
                )
                second = jnp.where(quad == 8 * g + rows + r, put, second)
            whole = jnp.sum(whole, axis=1, keepdims=True)
            second = jnp.where(lane == 32 * g + 3, whole, second)
        pk_out[w, 0] = first
        pk_out[w, 1] = second

    for mine, t2, s2 in peers:
        src_ref, dst_ref = pk_out.at[t2 * group + s2], pk.at[sub, tier]
        if mine:
            pltpu.make_async_copy(src_ref, dst_ref, r_pk).start()
        else:
            pltpu.make_async_remote_copy(
                src_ref=src_ref, dst_ref=dst_ref, send_sem=s_pk, recv_sem=r_pk,
                device_id=there(t2, s2), device_id_type=MESH,
            ).start()
    spread(m_hbm, col_m, beside, sub * rows + beside, 1, s_m, r_bm.at[sub])
    spread(t_hbm, col_t, beside, sub * rows + beside, 1, s_t, r_bt.at[sub])
    spread(m_hbm, col_m, inmost, sub * rows + inmost, 1, s_m, r_im)
    spread(t_hbm, col_t, inmost, sub * rows + inmost, 1, s_t, r_it)
    spread(m_hbm, col_m, other, sub * rows + other, 1, s_m, r_om.at[sub])
    spread(t_hbm, col_t, other, sub * rows + other, 1, s_t, r_rt.at[sub])

    has_low = place > 0
    has_high = place < ngrp - 1

    @pl.when(jnp.logical_not(has_low))
    def _():
        for ref in (halo_t, halo_m, halo_p, halo_1):
            ref[0] = jnp.zeros(ref.shape[1:], ref.dtype)

    @pl.when(jnp.logical_not(has_high))
    def _():
        for ref in (halo_t, halo_m, halo_p, halo_1):
            ref[1] = jnp.zeros(ref.shape[1:], ref.dtype)

    def halo(low_src, high_src, dst, which):
        down = pltpu.make_async_remote_copy(
            src_ref=low_src, dst_ref=dst.at[1],
            send_sem=s_h.at[which, 0], recv_sem=r_h.at[which, 1],
            device_id={"tile": lax.max(tile - group, sub)}, device_id_type=MESH,
        )
        up = pltpu.make_async_remote_copy(
            src_ref=high_src, dst_ref=dst.at[0],
            send_sem=s_h.at[which, 1], recv_sem=r_h.at[which, 0],
            device_id={"tile": lax.min(tile + group, ntile - group + sub)}, device_id_type=MESH,
        )
        return down, up

    def halo_recv(copies):
        pl.when(has_low)(lambda: copies[1].wait_recv())
        pl.when(has_high)(lambda: copies[0].wait_recv())

    def halo_sent(copies):
        pl.when(has_low)(lambda: copies[0].wait_send())
        pl.when(has_high)(lambda: copies[1].wait_send())

    h_t = halo(col_t.at[0], col_t.at[grows - 1], halo_t, 0)
    h_m = halo(col_m.at[0], col_m.at[grows - 1], halo_m, 1)
    h_p = halo(pk.at[0, :, 0], pk.at[group - 1, :, 0], halo_p, 2)
    h_1 = halo(t1.at[0], t1.at[grows - 1], halo_1, 3)

    all_but_one(p1g, r_p1g)
    p1z[0] = jnp.zeros(p1z.shape[1:], jnp.float32)
    for t in range(ntier):
        acc = p1g[t * group]
        for s in range(1, group):
            acc = acc + p1g[t * group + s]
        p1z[0, t : t + 1, :] = acc
    pl.when(has_high)(lambda: pl.semaphore_wait(entered, ngrp - 1 - place))
    across_send(p1z, s_p1z, r_p1z)

    for s, row in ((0, 0), (group - 1, grows - 1)):
        wait_for(col_t.at[row], r_et.at[s])
        wait_for(col_m.at[row], r_em.at[s])
    pl.when(has_low)(lambda: (h_m[0].start(), h_t[0].start()) and None)
    pl.when(has_high)(lambda: (h_m[1].start(), h_t[1].start()) and None)
    wait_for(pk, r_pk)
    pl.when(has_low)(lambda: h_p[0].start())
    pl.when(has_high)(lambda: h_p[1].start())

    inverse = 1.0 / ((2.0 * RATE) * rates[...])
    table = [
        [jnp.broadcast_to(inverse[a : a + 1, m : m + 1], (1, C)) for m in range(nmat)]
        for a in range(2)
    ]

    def lookup(codes, axes):
        outs = [jnp.broadcast_to(table[a][0], codes.shape) for a in axes]
        for m in range(1, nmat):
            hit = codes == m
            outs = [jnp.where(hit, table[a][m], o) for a, o in zip(axes, outs)]
        return outs

    def unpack(low, high, shift_low, shift_high, split):
        pieces = []
        for t in range(ntier):
            for g in range(lev // 8):
                a = roll(low(t), shift_low - 32 * g)
                if high is not None:
                    a = jnp.where(lane < split, a, roll(high(t), shift_high - 32 * g))
                pieces.append(a)
        return jnp.concatenate(pieces, axis=0)

    def swap(x):
        return jnp.where((lane & 3) == 1, roll(x, -1), roll(x, 1))

    half = 4 * rows
    out_t = unpack(lambda t: pk[0, t, 0], lambda t: pk[1, t, 0], 0, half, half)
    out_m = unpack(lambda t: pk[0, t, 0], lambda t: pk[1, t, 0], -half, 0, half)
    own_t = unpack(lambda t: pk[0, t, 1], lambda t: pk[1, t, 1], 0, half, half)
    own_m = unpack(lambda t: pk[0, t, 1], lambda t: pk[1, t, 1], -half, 0, half)
    ixc, iyc = lookup(out_m, (0, 1))
    (iyo,) = lookup(own_m, (1,))
    pos_low = (lane & 3) == 1

    op_active = [a_in[:, a : a + 1] for a in active_rows]
    op = jnp.concatenate(split(a_in[...]), axis=0)

    there_is = jnp.where(pos_low, jnp.where(own > 0, 1.0, 0.0), jnp.where(own < nwin - 1, 1.0, 0.0))
    c_in = there_is / (iyc + swap(iyo))
    c_far = 1.0 / (iyc + jnp.where(pos_low, roll(iyc, 1), roll(iyc, -1)))
    into_side = c_in * (swap(own_t) - out_t)
    spun_c = swap(c_in)
    kx = {}

    def conduct(r):
        kx[r], iy = lookup(col_m[r], (0, 1))
        ce[r] = roll(spun_c, -(4 * r + 2))
        cy[r] = jnp.where(lane == C - 1, ce[r], 1.0 / (iy + roll(iy, -1)))
        for q in (r, r + 1):
            if q - 1 in kx and q in kx:
                cx[q] = 1.0 / (kx[q - 1] + kx[q])

    outer = [0, grows - 1]
    near = [1, grows - 2]
    middle = list(range(2, grows - 2))
    for r in outer:
        conduct(r)
    for s, r in ((0, 1), (group - 1, grows - 2)):
        wait_for(col_m.at[r], r_bm.at[s])
        conduct(r)
    wait_for(col_m.at[pl.ds(rows - 1, 2)], r_im)
    for r in (rows - 1, rows):
        conduct(r)

    all_but_one(p1z, r_p1z)
    whole = total(p1z)
    count = whole[0:1, nblk : 2 * nblk]
    power = stat[...] * jnp.exp(fac[...] * whole[0:ntier, 0:nblk] / count)

    def label_of(s, w):
        return jnp.sum(jnp.where(note == 2 * nblk + w, p1g[s], 0.0), axis=1, keepdims=True)

    blkf = blk.astype(jnp.float32)

    def gain_of(pw, label):
        return SOURCE_GAIN * jnp.sum(jnp.where(blkf == label, pw, 0.0), axis=1, keepdims=True)

    own_labels = [label_of(s, own) for s in range(group)]
    gains = [gain_of(power, label) for label in own_labels]
    lift = []
    for s in range(group):
        acc = op_active[0] * gains[s][0:1, :]
        for t in range(1, ntier):
            acc = acc + op_active[t] * gains[s][t : t + 1, :]
        lift.append(acc)
    side = jnp.zeros((ntier, C), jnp.float32)
    for s in range(group):
        gl = gain_of(power, label_of(s, own - 1))
        gr = gain_of(power, label_of(s, own + 1))
        side = jnp.where(lane // half == s, jnp.where(pos_low, gl, gr), side)
    lift_c = op_active[0] * side[0:1, :]
    for t in range(1, ntier):
        lift_c = lift_c + op_active[t] * side[t : t + 1, :]

    first, last = kx[0], kx[grows - 1]

    def lateral(field, outside, r, above, below):
        here = field[r]
        edge_in = roll(outside, -(4 * r + 2))
        beside = jnp.where(lane == C - 1, edge_in, roll(here, -1))
        flux = cy[r] * (beside - here)
        left = jnp.where(lane == 0, ce[r] * (here - edge_in), roll(flux, 1))
        moved = here + (flux - left)
        return moved + cx[r + 1] * (below - here) - cx[r] * (here - above)

    halo_recv(h_m)
    (ix,) = lookup(halo_m[0], (0,))
    cx[0] = jnp.where(has_low, 1.0 / (ix + first), 0.0)
    (ix,) = lookup(halo_m[1], (0,))
    cx[grows] = jnp.where(has_high, 1.0 / (ix + last), 0.0)

    halo_recv(h_t)
    spun = swap(out_t)
    place_of = {r: i for i, r in enumerate(outer + [grows] + near + middle)}

    def at(r, n=1):
        return slice(place_of[r] * C, (place_of[r] + n) * C)

    def first_move(r):
        above = halo_t[0] if r == 0 else col_t[r - 1]
        below = halo_t[1] if r == grows - 1 else col_t[r + 1]
        mv[:, at(r)] = lateral(col_t, spun, r, above, below)

    for s, r in ((0, 1), (group - 1, grows - 2)):
        wait_for(col_t.at[r], r_bt.at[s])
    for r in outer:
        first_move(r)
    both = solve(op, mv[:, at(0, 2)])
    for i, r in enumerate(outer):
        t1[r] = both[:, i * C : (i + 1) * C] + lift[r // rows]
    pl.when(has_low)(lambda: h_1[0].start())
    pl.when(has_high)(lambda: h_1[1].start())

    halo_recv(h_p)
    end = 4 * (rows - 1)
    up_t = unpack(lambda t: halo_p[0, t], None, -end, 0, 0)
    up_m = unpack(lambda t: halo_p[0, t], None, -end - half, 0, 0)
    dn_t = unpack(lambda t: halo_p[1, t], None, 4 * (grows - 1), 0, 0)
    dn_m = unpack(lambda t: halo_p[1, t], None, 4 * (grows - 1) - half, 0, 0)
    (up_ix,) = lookup(up_m, (0,))
    (dn_ix,) = lookup(dn_m, (0,))
    at_top = lane < 4
    at_bottom = lane >= 4 * (grows - 1)
    up_c = 1.0 / (ixc + jnp.where(at_top, up_ix, roll(ixc, 4)))
    up_c = jnp.where(jnp.logical_and(at_top, jnp.logical_not(has_low)), 0.0, up_c)
    dn_c = 1.0 / (ixc + jnp.where(at_bottom, dn_ix, roll(ixc, -4)))
    dn_c = jnp.where(jnp.logical_and(at_bottom, jnp.logical_not(has_high)), 0.0, dn_c)
    part = (
        out_t
        + up_c * (jnp.where(at_top, up_t, roll(out_t, 4)) - out_t)
        + dn_c * (jnp.where(at_bottom, dn_t, roll(out_t, -4)) - out_t)
        + into_side
        + c_far * (jnp.where(pos_low, roll(out_t, 1), roll(out_t, -1)) - out_t)
    )


    mv[:, at(grows)] = part


    wait_for(col_t.at[pl.ds(rows - 1, 2)], r_it)
    flows = [
        cx[0] * (halo_t[0] - col_t[0]),
        cx[rows] * (col_t[rows] - col_t[rows - 1]),
        cx[grows] * (halo_t[1] - col_t[grows - 1]),
    ]
    inflow = (flows[0] + flows[1], flows[2] - flows[1])
    side_lane = jnp.logical_or((lane & 3) == 1, (lane & 3) == 2)
    stock = []
    for s in range(group):
        mine = jnp.logical_and(lane // half == s, side_lane)
        stock.append(
            inflow[s]
            - jnp.where(mine, into_side, 0.0)
            + jnp.where(lane == s * half + 3, own_t, 0.0)
        )
    n_act = -(-ntier // 8) * 8
    act = jnp.concatenate(
        [a_in[a : a + 1, :] for a in active_rows]
        + [jnp.zeros((n_act - ntier, levels), jnp.float32)], axis=0
    )
    found = solve(jnp.concatenate(split(act), axis=0), jnp.concatenate(stock, axis=1))
    slot = place * nwin + own
    note2 = lax.broadcasted_iota(jnp.int32, p2.shape[1:], 1)
    line = jnp.zeros(p2.shape[1:], jnp.float32)
    for s in range(group):
        acc = jnp.sum(found[0:ntier, s * C : (s + 1) * C], axis=1, keepdims=True)
        acc = acc + float(rows * C) * jnp.concatenate(
            [lift[s][a : a + 1, :] for a in active_rows], axis=0
        )
        name = own_labels[s].astype(jnp.int32)
        for t in range(ntier):
            line = line + jnp.where(note2 == t * nblk + name, acc[t : t + 1, :], 0.0)
    p2[slot] = line

    def to_all(t2, tile2):
        pltpu.make_async_remote_copy(
            src_ref=p2.at[slot], dst_ref=p2.at[slot], send_sem=s_p2, recv_sem=r_p2,
            device_id={"tier": t2, "tile": tile2}, device_id_type=MESH,
        ).start()

    def to_group(k, carry):
        for _, t2, s2 in peers:
            to_all(t2, lax.rem(base + k * group, ntile) + s2)
        return carry

    lax.fori_loop(1, ngrp, to_group, 0)
    for mine, t2, s2 in peers:
        if not mine:
            to_all(t2, base + s2)

    for s, r in ((0, rows - 2), (group - 1, rows + 1)):
        wait_for(col_m.at[r], r_om.at[s])
        conduct(r)

    for s, row in ((0, rows - 2), (group - 1, rows + 1)):
        wait_for(col_t.at[row], r_rt.at[s])
    for r in near + middle:
        first_move(r)
    most = solve(op, mv[:, at(grows, grows - 1)])
    for i, r in enumerate(near + middle):
        t1[r] = most[:, (i + 1) * C : (i + 2) * C] + lift[r // rows]
    t1c = most[:, :C] + lift_c

    own_tile, next_tile = peers[-ntier:], peers[:-ntier]

    def send_rows(first_low, first_high, count):
        to_own = lax.select(sub == 0, first_low, first_high)
        to_next = lax.select(sub == 0, first_high, first_low)
        for whom, row in ((next_tile, to_next), (own_tile, to_own)):
            for mine, t2, s2 in whom:
                src_ref = res.at[pl.ds(row, count), levs(t2), :]
                dst_ref = out.at[pl.ds(row - s2 * rows, count), :, cols(own)]
                if mine:
                    pltpu.make_async_copy(src_ref, dst_ref, r_o).start()
                else:
                    pltpu.make_async_remote_copy(
                        src_ref=src_ref, dst_ref=dst_ref, send_sem=s_o, recv_sem=r_o,
                        device_id=there(t2, s2), device_id_type=MESH,
                    ).start()

    spun = swap(t1c)

    def finish(rs):
        for r in rs:
            above = halo_1[0] if r == 0 else t1[r - 1]
            below = halo_1[1] if r == grows - 1 else t1[r + 1]
            mv[:, at(r)] = lateral(t1, spun, r, above, below)
        x = solve(op, mv[:, at(rs[0], len(rs))])
        for i, r in enumerate(rs):
            res[r] = x[:, i * C : (i + 1) * C]

    finish(middle)
    send_rows(2, rows, rows - 2)
    finish(near)
    halo_recv(h_1)
    finish(outer)
    send_rows(0, grows - 2, 2)

    all_but_one(p2, r_p2)
    whole = jnp.sum(p2[...], axis=0)
    whole = jnp.concatenate([whole[:, t * nblk : (t + 1) * nblk] for t in range(ntier)], axis=0)
    power = stat[...] * jnp.exp(fac[...] * whole[0:ntier, 0:nblk] / count)
    mine = lax.broadcasted_iota(jnp.int32, (ntier, nblk), 0) == tier
    pw_out[...] = jnp.sum(jnp.where(mine, power, 0.0), axis=0, keepdims=True)
    own_op = a_in[levs(tier), :]
    for j in range(width // C):
        g = SOURCE_GAIN * jnp.sum(jnp.where(blk == labels[0, j], power, 0.0), axis=1, keepdims=True)
        acc = own_op[:, active_rows[0] : active_rows[0] + 1] * g[0:1, :]
        for t in range(1, ntier):
            a = active_rows[t]
            acc = acc + own_op[:, a : a + 1] * g[t : t + 1, :]
        lift_out[:, j * C : (j + 1) * C] = jnp.broadcast_to(acc, (lev, C))
    wait_for(out, r_o)

    for copies in (h_t, h_m, h_p, h_1):
        halo_sent(copies)
    sent = pl.ds(0, nwin - 1)
    wait_for(res.at[sent], s_t)
    wait_for(res.at[sent], s_m)
    wait_for(res.at[sent], s_o)
    wait_for(pk_out.at[sent], s_pk)
    all_but_one(p1g, s_p1g)
    all_but_one(p1z, s_p1z)
    all_but_one(p2, s_p2)


def last(field, lift, power, out, power_out, done, sem):
    copies = []
    for r in range(field.shape[0]):
        done[r] = field[r] + lift[...]
        copies.append(pltpu.make_async_copy(done.at[r], out.at[r], sem.at[r]))
        copies[-1].start()
    copies.append(pltpu.make_async_copy(power, power_out, sem.at[field.shape[0]]))
    copies[-1].start()
    for copy in copies:
        copy.wait()


def solution(mesh):
    ntier, ntile = mesh.shape["tier"], mesh.shape["tile"]

    def shards(temp, mats, rates, labels, stat, fac, op):
        rows, lev, width = temp.shape
        nblk = stat.shape[1]
        pad = lambda n: -(-n // C) * C
        group = width // (ntier * C)
        levels, grows, ngrp, nwin = lev * ntier, rows * group, ntile // group, width // C
        f32, i32 = jnp.float32, jnp.int32
        vm = lambda shape, dtype=f32: pltpu.VMEM(shape, dtype)
        dma = pltpu.SemaphoreType.DMA
        vmem = pl.BlockSpec(memory_space=pltpu.VMEM)
        block = (grows, levels, C)
        args = (temp, mats, rates, labels, stat, fac, op)
        args = [pltpu.with_memory_space_constraint(x, pltpu.HBM) for x in args]
        field, power, lift = pl.pallas_call(
            functools.partial(kernel, ntier, ntile, nblk, group),
            out_shape=(vm(temp.shape), vm((1, nblk)), vm((lev, width))),
            in_specs=[pl.BlockSpec(memory_space=pltpu.HBM)] * 7,
            out_specs=(pl.BlockSpec(memory_space=pl.ANY), vmem, vmem),
            scratch_shapes=[
                vm(temp.shape), vm(mats.shape, i32), vm(rates.shape),
                pltpu.SMEM(labels.shape, i32), vm(stat.shape), vm(fac.shape), vm(op.shape),
                dma((7,)),
                vm(block), vm(block, i32), vm((2, levels, C)), vm((2, levels, C), i32), vm((2, levels, C)),
                vm((nwin, 2, 8, C)), vm((group, ntier, 2, 8, C)), vm((2, ntier, 8, C)),
                vm((grows + 1, levels, C)), vm(block), vm(block), vm((levels, (grows + 1) * C)),
                vm(block), vm((levels, C)), vm(block),
                vm((nwin, 1, pad(2 * nblk + nwin))), vm((ngrp, 8, pad(2 * nblk + nwin))),
                vm((ngrp * nwin, 1, pad(ntier * nblk))),
                dma, dma, dma, dma,
                dma((group,)), dma((group,)), dma((group,)), dma((group,)), dma, dma, dma((group,)),
                dma((group,)), dma, dma,
                dma((4, 2)), dma((4, 2)),
                dma, dma, dma, dma, dma, dma, pltpu.SemaphoreType.REGULAR,
            ],
            compiler_params=pltpu.CompilerParams(
                collective_id=0, has_side_effects=True, vmem_limit_bytes=48 * 1024 * 1024
            ),
        )(*args)
        anywhere = pl.BlockSpec(memory_space=pltpu.HBM)
        return pl.pallas_call(
            last,
            out_shape=(
                jax.ShapeDtypeStruct(temp.shape, f32),
                jax.ShapeDtypeStruct((1, nblk), f32),
            ),
            in_specs=[vmem] * 3,
            out_specs=(anywhere, anywhere),
            scratch_shapes=[vm(temp.shape), dma((rows + 1,))],
            compiler_params=pltpu.CompilerParams(vmem_limit_bytes=4 * 1024 * 1024),
        )(field, lift, power)

    return jax.shard_map(
        shards,
        mesh=mesh,
        in_specs=(P("tile", "tier", None), P("tile", "tier", None), P(), P("tile", None), P(), P(), P()),
        out_specs=(P("tile", "tier", None), P("tier", None)),
        check_vma=False,
    )
```

```python
import functools

import jax
import jax.numpy as jnp
from jax import lax
from jax.experimental import pallas as pl
from jax.experimental.pallas import tpu as pltpu
from jax.sharding import PartitionSpec as P

C = 128
RATE = 0.12
SOURCE_GAIN = 0.02
MESH = pl.DeviceIdType.MESH


def split(x):
    high = x.astype(jnp.bfloat16)
    return high, (x - high.astype(jnp.float32)).astype(jnp.bfloat16)


def solve(op, x):
    high, low = split(x)
    n = op.shape[0] // 2
    both = jnp.dot(op, high, preferred_element_type=jnp.float32)
    more = jnp.dot(op[:n], low, preferred_element_type=jnp.float32)
    return both[:n] + (both[n:] + more)


def roll(x, shift):
    return pltpu.roll(x, shift % C, x.ndim - 1) if shift % C else x


def kernel(
    ntier, ntile, nblk, group,
    t_hbm, m_hbm, rates_hbm, labels_hbm, stat_hbm, fac_hbm, a_hbm,
    out, pw_out, lift_out,
    t_in, m_in, rates, labels, stat, fac, a_in, s_in,
    col_t, col_m, halo_t, halo_m, halo_1,
    pk_out, pk, halo_p,
    cx, cy, ce, mv, t1, t1c, res,
    p1g, p1z, p2,
    s_t, s_m, s_pk, s_o,
    r_et, r_em, r_bt, r_bm, r_it, r_im, r_om, r_rt, r_pk, r_o,
    s_h, r_h,
    s_p1g, r_p1g, s_p1z, r_p1z, s_p2, r_p2, entered,
):
    tier = lax.axis_index("tier")
    tile = lax.axis_index("tile")
    rows, lev, width = t_in.shape
    levels = lev * ntier
    nmat = rates.shape[1]
    ngrp = ntile // group
    grows = rows * group
    sub = lax.rem(tile, group)
    base = tile - sub
    place = tile // group
    own = tier * group + sub
    nwin = ntier * group
    active_rows = [t * lev for t in range(ntier)]

    loads = [
        pltpu.make_async_copy(src, dst, s_in.at[i])
        for i, (src, dst) in enumerate(
            ((t_hbm, t_in), (m_hbm, m_in), (labels_hbm, labels), (rates_hbm, rates),
             (stat_hbm, stat), (fac_hbm, fac), (a_hbm, a_in))
        )
    ]
    for load in loads:
        load.start()

    turned = tier + 1 - 2 * lax.rem(tier, 2)
    peers = []
    for b in range(group - 1, -1, -1):
        for a in range(ntier - 2, -1, -2):
            for start in (tier, turned):
                mine = a == 0 and b == 0 and start is tier
                peers.append((mine, lax.rem(start + a, ntier), lax.rem(sub + b, group)))

    def there(t2, s2):
        return {"tier": t2, "tile": base + s2}

    barrier = pltpu.get_barrier_semaphore()
    for mine, t2, s2 in peers:
        if not mine:
            pl.semaphore_signal(barrier, inc=1, device_id=there(t2, s2), device_id_type=MESH)

    def across(k):
        return {"tile": lax.rem(tile + k * group, ntile)}

    def greet(sem, low, high):
        def one(k, carry):
            pl.semaphore_signal(
                sem, inc=1, device_id={"tile": k * group + sub}, device_id_type=MESH
            )
            return carry

        lax.fori_loop(low, high, one, 0)

    greet(barrier, place + 1, ngrp)

    def cols(w):
        return pl.ds(pl.multiple_of(w * C, C), C)

    def levs(t):
        return pl.ds(pl.multiple_of(t * lev, 8), lev)

    lane = lax.broadcasted_iota(jnp.int32, (1, C), 1)
    blk = lax.broadcasted_iota(jnp.int32, (1, nblk), 1)

    for load in loads:
        load.wait()

    note = lax.broadcasted_iota(jnp.int32, p1g.shape[1:], 1)
    line = jnp.zeros(p1g.shape[1:], jnp.float32)
    active = t_in[0, 0:1, :]
    for r in range(1, rows):
        active = active + t_in[r, 0:1, :]
    for j in range(width // C):
        label = labels[0, j]
        part = jnp.sum(active[:, j * C : (j + 1) * C], axis=1, keepdims=True)
        line = line + jnp.where(note == label, part, 0.0)
        line = line + jnp.where(note == nblk + label, float(rows * C), 0.0)
        line = jnp.where(note == 2 * nblk + j, label.astype(jnp.float32), line)
    p1g[own] = line

    pl.semaphore_wait(barrier, nwin - 1 + place)
    greet(entered, 0, place)

    def group_send(buf, s_sem, r_sem):
        for mine, t2, s2 in peers:
            if not mine:
                pltpu.make_async_remote_copy(
                    src_ref=buf.at[own], dst_ref=buf.at[own], send_sem=s_sem, recv_sem=r_sem,
                    device_id=there(t2, s2), device_id_type=MESH,
                ).start()

    def across_send(buf, s_sem, r_sem):
        def send(k, carry):
            pltpu.make_async_remote_copy(
                src_ref=buf.at[0], dst_ref=buf.at[k], send_sem=s_sem, recv_sem=r_sem,
                device_id=across(k), device_id_type=MESH,
            ).start()
            return carry

        lax.fori_loop(1, ngrp, send, 0)

    def wait_for(ref, sem):
        pltpu.make_async_copy(ref, ref, sem).wait()

    def all_but_one(buf, sem):
        wait_for(buf.at[pl.ds(1, buf.shape[0] - 1)], sem)

    def total(buf):
        return lax.fori_loop(1, ngrp, lambda k, acc: acc + buf[k], buf[0])

    group_send(p1g, s_p1g, r_p1g)

    def spread(src, dst, row, to, count, s_sem, r_sem):
        for mine, t2, s2 in peers:
            src_ref = src.at[pl.ds(row, count), :, cols(t2 * group + s2)]
            dst_ref = dst.at[pl.ds(to, count), levs(tier), :]
            if mine:
                pltpu.make_async_copy(src_ref, dst_ref, r_sem).start()
            else:
                pltpu.make_async_remote_copy(
                    src_ref=src_ref, dst_ref=dst_ref, send_sem=s_sem, recv_sem=r_sem,
                    device_id=there(t2, s2), device_id_type=MESH,
                ).start()

    edge = lax.select(sub == 0, 0, rows - 1)
    beside = lax.select(sub == 0, 1, rows - 2)
    other = lax.select(sub == 0, rows - 2, 1)
    inmost = lax.select(sub == 0, rows - 1, 0)
    spread(t_hbm, col_t, edge, sub * rows + edge, 1, s_t, r_et.at[sub])
    spread(m_hbm, col_m, edge, sub * rows + edge, 1, s_m, r_em.at[sub])

    quad = lane >> 2
    for w in range(nwin):
        low = max(w - 1, 0) * C
        high = min(w + 1, nwin - 1) * C
        first = second = None
        for g in range(lev // 8):
            ls = slice(8 * g, 8 * g + 8)
            for q, src in ((0, t_in), (rows, m_in)):
                for r in range(rows):
                    both = jnp.where(
                        lane >= 64, src[r, ls, low : low + C], src[r, ls, high : high + C]
                    )
                    if q:
                        both = both.astype(jnp.float32)
                    put = roll(both, 32 * g + 4 * (q + r) + 2)
                    first = put if first is None else jnp.where(quad == 8 * g + q + r, put, first)
            whole = None
            for r in range(rows):
                block = t_in[r, ls, w * C : (w + 1) * C]
                whole = block if whole is None else whole + block
                put = roll(block, 32 * g + 4 * r + 2)
                second = put if second is None else jnp.where(quad == 8 * g + r, put, second)
                put = roll(
                    m_in[r, ls, w * C : (w + 1) * C].astype(jnp.float32), 32 * g + 4 * (rows + r) + 2
                )
                second = jnp.where(quad == 8 * g + rows + r, put, second)
            whole = jnp.sum(whole, axis=1, keepdims=True)
            second = jnp.where(lane == 32 * g + 3, whole, second)
        pk_out[w, 0] = first
        pk_out[w, 1] = second

    for mine, t2, s2 in peers:
        src_ref, dst_ref = pk_out.at[t2 * group + s2], pk.at[sub, tier]
        if mine:
            pltpu.make_async_copy(src_ref, dst_ref, r_pk).start()
        else:
            pltpu.make_async_remote_copy(
                src_ref=src_ref, dst_ref=dst_ref, send_sem=s_pk, recv_sem=r_pk,
                device_id=there(t2, s2), device_id_type=MESH,
            ).start()
    spread(m_hbm, col_m, beside, sub * rows + beside, 1, s_m, r_bm.at[sub])
    spread(t_hbm, col_t, beside, sub * rows + beside, 1, s_t, r_bt.at[sub])
    spread(m_hbm, col_m, inmost, sub * rows + inmost, 1, s_m, r_im)
    spread(t_hbm, col_t, inmost, sub * rows + inmost, 1, s_t, r_it)
    spread(m_hbm, col_m, other, sub * rows + other, 1, s_m, r_om.at[sub])
    spread(t_hbm, col_t, other, sub * rows + other, 1, s_t, r_rt.at[sub])

    has_low = place > 0
    has_high = place < ngrp - 1

    @pl.when(jnp.logical_not(has_low))
    def _():
        for ref in (halo_t, halo_m, halo_p, halo_1):
            ref[0] = jnp.zeros(ref.shape[1:], ref.dtype)

    @pl.when(jnp.logical_not(has_high))
    def _():
        for ref in (halo_t, halo_m, halo_p, halo_1):
            ref[1] = jnp.zeros(ref.shape[1:], ref.dtype)

    def halo(low_src, high_src, dst, which):
        down = pltpu.make_async_remote_copy(
            src_ref=low_src, dst_ref=dst.at[1],
            send_sem=s_h.at[which, 0], recv_sem=r_h.at[which, 1],
            device_id={"tile": lax.max(tile - group, sub)}, device_id_type=MESH,
        )
        up = pltpu.make_async_remote_copy(
            src_ref=high_src, dst_ref=dst.at[0],
            send_sem=s_h.at[which, 1], recv_sem=r_h.at[which, 0],
            device_id={"tile": lax.min(tile + group, ntile - group + sub)}, device_id_type=MESH,
        )
        return down, up

    def halo_recv(copies):
        pl.when(has_low)(lambda: copies[1].wait_recv())
        pl.when(has_high)(lambda: copies[0].wait_recv())

    h_t = halo(col_t.at[0], col_t.at[grows - 1], halo_t, 0)
    h_m = halo(col_m.at[0], col_m.at[grows - 1], halo_m, 1)
    h_p = halo(pk.at[0, :, 0], pk.at[group - 1, :, 0], halo_p, 2)
    h_1 = halo(t1.at[0], t1.at[grows - 1], halo_1, 3)

    all_but_one(p1g, r_p1g)
    p1z[0] = jnp.zeros(p1z.shape[1:], jnp.float32)
    for t in range(ntier):
        acc = p1g[t * group]
        for s in range(1, group):
            acc = acc + p1g[t * group + s]
        p1z[0, t : t + 1, :] = acc
    pl.when(has_high)(lambda: pl.semaphore_wait(entered, ngrp - 1 - place))
    across_send(p1z, s_p1z, r_p1z)

    for s, row in ((0, 0), (group - 1, grows - 1)):
        wait_for(col_t.at[row], r_et.at[s])
        wait_for(col_m.at[row], r_em.at[s])
    pl.when(has_low)(lambda: (h_m[0].start(), h_t[0].start()) and None)
    pl.when(has_high)(lambda: (h_m[1].start(), h_t[1].start()) and None)
    wait_for(pk, r_pk)
    pl.when(has_low)(lambda: h_p[0].start())
    pl.when(has_high)(lambda: h_p[1].start())

    inverse = 1.0 / ((2.0 * RATE) * rates[...])
    table = [
        [jnp.broadcast_to(inverse[a : a + 1, m : m + 1], (1, C)) for m in range(nmat)]
        for a in range(2)
    ]

    def lookup(codes, axes):
        outs = [jnp.broadcast_to(table[a][0], codes.shape) for a in axes]
        for m in range(1, nmat):
            hit = codes == m
            outs = [jnp.where(hit, table[a][m], o) for a, o in zip(axes, outs)]
        return outs

    def unpack(low, high, shift_low, shift_high, split):
        pieces = []
        for t in range(ntier):
            for g in range(lev // 8):
                a = roll(low(t), shift_low - 32 * g)
                if high is not None:
                    a = jnp.where(lane < split, a, roll(high(t), shift_high - 32 * g))
                pieces.append(a)
        return jnp.concatenate(pieces, axis=0)

    def swap(x):
        return jnp.where((lane & 3) == 1, roll(x, -1), roll(x, 1))

    half = 4 * rows
    out_t = unpack(lambda t: pk[0, t, 0], lambda t: pk[1, t, 0], 0, half, half)
    out_m = unpack(lambda t: pk[0, t, 0], lambda t: pk[1, t, 0], -half, 0, half)
    own_t = unpack(lambda t: pk[0, t, 1], lambda t: pk[1, t, 1], 0, half, half)
    own_m = unpack(lambda t: pk[0, t, 1], lambda t: pk[1, t, 1], -half, 0, half)
    ixc, iyc = lookup(out_m, (0, 1))
    (iyo,) = lookup(own_m, (1,))
    pos_low = (lane & 3) == 1

    op_active = [a_in[:, a : a + 1] for a in active_rows]
    op = jnp.concatenate(split(a_in[...]), axis=0)

    there_is = jnp.where(pos_low, jnp.where(own > 0, 1.0, 0.0), jnp.where(own < nwin - 1, 1.0, 0.0))
    c_in = there_is / (iyc + swap(iyo))
    c_far = 1.0 / (iyc + jnp.where(pos_low, roll(iyc, 1), roll(iyc, -1)))
    into_side = c_in * (swap(own_t) - out_t)
    spun_c = swap(c_in)
    kx = {}

    def conduct(r):
        kx[r], iy = lookup(col_m[r], (0, 1))
        ce[r] = roll(spun_c, -(4 * r + 2))
        cy[r] = jnp.where(lane == C - 1, ce[r], 1.0 / (iy + roll(iy, -1)))
        for q in (r, r + 1):
            if q - 1 in kx and q in kx:
                cx[q] = 1.0 / (kx[q - 1] + kx[q])

    outer = [0, grows - 1]
    near = [1, grows - 2]
    middle = list(range(2, grows - 2))
    for r in outer:
        conduct(r)
    for s, r in ((0, 1), (group - 1, grows - 2)):
        wait_for(col_m.at[r], r_bm.at[s])
        conduct(r)
    wait_for(col_m.at[pl.ds(rows - 1, 2)], r_im)
    for r in (rows - 1, rows):
        conduct(r)

    all_but_one(p1z, r_p1z)
    whole = total(p1z)
    count = whole[0:1, nblk : 2 * nblk]
    power = stat[...] * jnp.exp(fac[...] * whole[0:ntier, 0:nblk] / count)

    def label_of(s, w):
        return jnp.sum(jnp.where(note == 2 * nblk + w, p1g[s], 0.0), axis=1, keepdims=True)

    blkf = blk.astype(jnp.float32)

    def gain_of(pw, label):
        return SOURCE_GAIN * jnp.sum(jnp.where(blkf == label, pw, 0.0), axis=1, keepdims=True)

    own_labels = [label_of(s, own) for s in range(group)]
    gains = [gain_of(power, label) for label in own_labels]
    lift = []
    for s in range(group):
        acc = op_active[0] * gains[s][0:1, :]
        for t in range(1, ntier):
            acc = acc + op_active[t] * gains[s][t : t + 1, :]
        lift.append(acc)
    side = jnp.zeros((ntier, C), jnp.float32)
    for s in range(group):
        gl = gain_of(power, label_of(s, own - 1))
        gr = gain_of(power, label_of(s, own + 1))
        side = jnp.where(lane // half == s, jnp.where(pos_low, gl, gr), side)
    lift_c = op_active[0] * side[0:1, :]
    for t in range(1, ntier):
        lift_c = lift_c + op_active[t] * side[t : t + 1, :]

    first, last = kx[0], kx[grows - 1]

    def lateral(field, outside, r, above, below):
        here = field[r]
        edge_in = roll(outside, -(4 * r + 2))
        beside = jnp.where(lane == C - 1, edge_in, roll(here, -1))
        flux = cy[r] * (beside - here)
        left = jnp.where(lane == 0, ce[r] * (here - edge_in), roll(flux, 1))
        moved = here + (flux - left)
        return moved + cx[r + 1] * (below - here) - cx[r] * (here - above)

    halo_recv(h_m)
    (ix,) = lookup(halo_m[0], (0,))
    cx[0] = jnp.where(has_low, 1.0 / (ix + first), 0.0)
    (ix,) = lookup(halo_m[1], (0,))
    cx[grows] = jnp.where(has_high, 1.0 / (ix + last), 0.0)

    halo_recv(h_t)
    spun = swap(out_t)
    place_of = {r: i for i, r in enumerate(outer + [grows] + near + middle)}

    def at(r, n=1):
        return slice(place_of[r] * C, (place_of[r] + n) * C)

    def first_move(r):
        above = halo_t[0] if r == 0 else col_t[r - 1]
        below = halo_t[1] if r == grows - 1 else col_t[r + 1]
        mv[:, at(r)] = lateral(col_t, spun, r, above, below)

    for s, r in ((0, 1), (group - 1, grows - 2)):
        wait_for(col_t.at[r], r_bt.at[s])
    for r in outer:
        first_move(r)
    both = solve(op, mv[:, at(0, 2)])
    for i, r in enumerate(outer):
        t1[r] = both[:, i * C : (i + 1) * C] + lift[r // rows]
    pl.when(has_low)(lambda: h_1[0].start())
    pl.when(has_high)(lambda: h_1[1].start())

    halo_recv(h_p)
    end = 4 * (rows - 1)
    up_t = unpack(lambda t: halo_p[0, t], None, -end, 0, 0)
    up_m = unpack(lambda t: halo_p[0, t], None, -end - half, 0, 0)
    dn_t = unpack(lambda t: halo_p[1, t], None, 4 * (grows - 1), 0, 0)
    dn_m = unpack(lambda t: halo_p[1, t], None, 4 * (grows - 1) - half, 0, 0)
    (up_ix,) = lookup(up_m, (0,))
    (dn_ix,) = lookup(dn_m, (0,))
    at_top = lane < 4
    at_bottom = lane >= 4 * (grows - 1)
    up_c = 1.0 / (ixc + jnp.where(at_top, up_ix, roll(ixc, 4)))
    up_c = jnp.where(jnp.logical_and(at_top, jnp.logical_not(has_low)), 0.0, up_c)
    dn_c = 1.0 / (ixc + jnp.where(at_bottom, dn_ix, roll(ixc, -4)))
    dn_c = jnp.where(jnp.logical_and(at_bottom, jnp.logical_not(has_high)), 0.0, dn_c)
    part = (
        out_t
        + up_c * (jnp.where(at_top, up_t, roll(out_t, 4)) - out_t)
        + dn_c * (jnp.where(at_bottom, dn_t, roll(out_t, -4)) - out_t)
        + into_side
        + c_far * (jnp.where(pos_low, roll(out_t, 1), roll(out_t, -1)) - out_t)
    )


    mv[:, at(grows)] = part


    wait_for(col_t.at[pl.ds(rows - 1, 2)], r_it)
    flows = [
        cx[0] * (halo_t[0] - col_t[0]),
        cx[rows] * (col_t[rows] - col_t[rows - 1]),
        cx[grows] * (halo_t[1] - col_t[grows - 1]),
    ]
    inflow = (flows[0] + flows[1], flows[2] - flows[1])
    side_lane = jnp.logical_or((lane & 3) == 1, (lane & 3) == 2)
    stock = []
    for s in range(group):
        mine = jnp.logical_and(lane // half == s, side_lane)
        stock.append(
            inflow[s]
            - jnp.where(mine, into_side, 0.0)
            + jnp.where(lane == s * half + 3, own_t, 0.0)
        )
    n_act = -(-ntier // 8) * 8
    act = jnp.concatenate(
        [a_in[a : a + 1, :] for a in active_rows]
        + [jnp.zeros((n_act - ntier, levels), jnp.float32)], axis=0
    )
    found = solve(jnp.concatenate(split(act), axis=0), jnp.concatenate(stock, axis=1))
    slot = place * nwin + own
    note2 = lax.broadcasted_iota(jnp.int32, p2.shape[1:], 1)
    line = jnp.zeros(p2.shape[1:], jnp.float32)
    for s in range(group):
        acc = jnp.sum(found[0:ntier, s * C : (s + 1) * C], axis=1, keepdims=True)
        acc = acc + float(rows * C) * jnp.concatenate(
            [lift[s][a : a + 1, :] for a in active_rows], axis=0
        )
        name = own_labels[s].astype(jnp.int32)
        for t in range(ntier):
            line = line + jnp.where(note2 == t * nblk + name, acc[t : t + 1, :], 0.0)
    p2[slot] = line

    def to_all(t2, tile2):
        pltpu.make_async_remote_copy(
            src_ref=p2.at[slot], dst_ref=p2.at[slot], send_sem=s_p2, recv_sem=r_p2,
            device_id={"tier": t2, "tile": tile2}, device_id_type=MESH,
        ).start()

    def to_group(k, carry):
        for _, t2, s2 in peers:
            to_all(t2, lax.rem(base + k * group, ntile) + s2)
        return carry

    lax.fori_loop(1, ngrp, to_group, 0)
    for mine, t2, s2 in peers:
        if not mine:
            to_all(t2, base + s2)

    for s, r in ((0, rows - 2), (group - 1, rows + 1)):
        wait_for(col_m.at[r], r_om.at[s])
        conduct(r)

    for s, row in ((0, rows - 2), (group - 1, rows + 1)):
        wait_for(col_t.at[row], r_rt.at[s])
    for r in near + middle:
        first_move(r)
    most = solve(op, mv[:, at(grows, grows - 1)])
    for i, r in enumerate(near + middle):
        t1[r] = most[:, (i + 1) * C : (i + 2) * C] + lift[r // rows]
    t1c = most[:, :C] + lift_c

    own_tile, next_tile = peers[-ntier:], peers[:-ntier]

    def send_rows(first_low, first_high, count):
        to_own = lax.select(sub == 0, first_low, first_high)
        to_next = lax.select(sub == 0, first_high, first_low)
        for whom, row in ((next_tile, to_next), (own_tile, to_own)):
            for mine, t2, s2 in whom:
                src_ref = res.at[pl.ds(row, count), levs(t2), :]
                dst_ref = out.at[pl.ds(row - s2 * rows, count), :, cols(own)]
                if mine:
                    pltpu.make_async_copy(src_ref, dst_ref, r_o).start()
                else:
                    pltpu.make_async_remote_copy(
                        src_ref=src_ref, dst_ref=dst_ref, send_sem=s_o, recv_sem=r_o,
                        device_id=there(t2, s2), device_id_type=MESH,
                    ).start()

    spun = swap(t1c)

    def finish(rs):
        for r in rs:
            above = halo_1[0] if r == 0 else t1[r - 1]
            below = halo_1[1] if r == grows - 1 else t1[r + 1]
            mv[:, at(r)] = lateral(t1, spun, r, above, below)
        x = solve(op, mv[:, at(rs[0], len(rs))])
        for i, r in enumerate(rs):
            res[r] = x[:, i * C : (i + 1) * C]

    finish(middle)
    send_rows(2, rows, rows - 2)
    finish(near)
    halo_recv(h_1)
    finish(outer)
    send_rows(0, grows - 2, 2)

    all_but_one(p2, r_p2)
    whole = jnp.sum(p2[...], axis=0)
    whole = jnp.concatenate([whole[:, t * nblk : (t + 1) * nblk] for t in range(ntier)], axis=0)
    power = stat[...] * jnp.exp(fac[...] * whole[0:ntier, 0:nblk] / count)
    mine = lax.broadcasted_iota(jnp.int32, (ntier, nblk), 0) == tier
    pw_out[...] = jnp.sum(jnp.where(mine, power, 0.0), axis=0, keepdims=True)
    own_op = a_in[levs(tier), :]
    for j in range(width // C):
        g = SOURCE_GAIN * jnp.sum(jnp.where(blk == labels[0, j], power, 0.0), axis=1, keepdims=True)
        acc = own_op[:, active_rows[0] : active_rows[0] + 1] * g[0:1, :]
        for t in range(1, ntier):
            a = active_rows[t]
            acc = acc + own_op[:, a : a + 1] * g[t : t + 1, :]
        lift_out[:, j * C : (j + 1) * C] = jnp.broadcast_to(acc, (lev, C))

    def passed(side):
        for copies in (h_t, h_m, h_p, h_1):
            copies[side].wait_send()

    pl.when(has_low)(lambda: passed(0))
    pl.when(has_high)(lambda: passed(1))
    sent = pl.ds(0, nwin - 1)
    wait_for(res.at[sent], s_t)
    wait_for(res.at[sent], s_m)
    wait_for(pk_out.at[sent], s_pk)
    all_but_one(p1g, s_p1g)
    all_but_one(p1z, s_p1z)
    all_but_one(p2, s_p2)
    wait_for(res.at[sent], s_o)
    wait_for(out, r_o)


def last(field, lift, power, out, power_out, done, sem):
    copies = []
    for r in range(field.shape[0]):
        done[r] = field[r] + lift[...]
        copies.append(pltpu.make_async_copy(done.at[r], out.at[r], sem.at[r]))
        copies[-1].start()
    copies.append(pltpu.make_async_copy(power, power_out, sem.at[field.shape[0]]))
    copies[-1].start()
    for copy in copies:
        copy.wait()


def solution(mesh):
    ntier, ntile = mesh.shape["tier"], mesh.shape["tile"]

    def shards(temp, mats, rates, labels, stat, fac, op):
        rows, lev, width = temp.shape
        nblk = stat.shape[1]
        pad = lambda n: -(-n // C) * C
        group = width // (ntier * C)
        levels, grows, ngrp, nwin = lev * ntier, rows * group, ntile // group, width // C
        f32, i32 = jnp.float32, jnp.int32
        vm = lambda shape, dtype=f32: pltpu.VMEM(shape, dtype)
        dma = pltpu.SemaphoreType.DMA
        vmem = pl.BlockSpec(memory_space=pltpu.VMEM)
        block = (grows, levels, C)
        args = (temp, mats, rates, labels, stat, fac, op)
        args = [pltpu.with_memory_space_constraint(x, pltpu.HBM) for x in args]
        field, power, lift = pl.pallas_call(
            functools.partial(kernel, ntier, ntile, nblk, group),
            out_shape=(vm(temp.shape), vm((1, nblk)), vm((lev, width))),
            in_specs=[pl.BlockSpec(memory_space=pltpu.HBM)] * 7,
            out_specs=(pl.BlockSpec(memory_space=pl.ANY), vmem, vmem),
            scratch_shapes=[
                vm(temp.shape), vm(mats.shape, i32), vm(rates.shape),
                pltpu.SMEM(labels.shape, i32), vm(stat.shape), vm(fac.shape), vm(op.shape),
                dma((7,)),
                vm(block), vm(block, i32), vm((2, levels, C)), vm((2, levels, C), i32), vm((2, levels, C)),
                vm((nwin, 2, 8, C)), vm((group, ntier, 2, 8, C)), vm((2, ntier, 8, C)),
                vm((grows + 1, levels, C)), vm(block), vm(block), vm((levels, (grows + 1) * C)),
                vm(block), vm((levels, C)), vm(block),
                vm((nwin, 1, pad(2 * nblk + nwin))), vm((ngrp, 8, pad(2 * nblk + nwin))),
                vm((ngrp * nwin, 1, pad(ntier * nblk))),
                dma, dma, dma, dma,
                dma((group,)), dma((group,)), dma((group,)), dma((group,)), dma, dma, dma((group,)),
                dma((group,)), dma, dma,
                dma((4, 2)), dma((4, 2)),
                dma, dma, dma, dma, dma, dma, pltpu.SemaphoreType.REGULAR,
            ],
            compiler_params=pltpu.CompilerParams(
                collective_id=0, has_side_effects=True, vmem_limit_bytes=48 * 1024 * 1024
            ),
        )(*args)
        anywhere = pl.BlockSpec(memory_space=pltpu.HBM)
        return pl.pallas_call(
            last,
            out_shape=(
                jax.ShapeDtypeStruct(temp.shape, f32),
                jax.ShapeDtypeStruct((1, nblk), f32),
            ),
            in_specs=[vmem] * 3,
            out_specs=(anywhere, anywhere),
            scratch_shapes=[vm(temp.shape), dma((rows + 1,))],
            compiler_params=pltpu.CompilerParams(vmem_limit_bytes=4 * 1024 * 1024),
        )(field, lift, power)

    return jax.shard_map(
        shards,
        mesh=mesh,
        in_specs=(P("tile", "tier", None), P("tile", "tier", None), P(), P("tile", None), P(), P(), P()),
        out_specs=(P("tile", "tier", None), P("tier", None)),
        check_vma=False,
    )
```
